256 devices in a mesh: rows: 32 (over x, z_lo, core), cent: 8 (over y, z_hi).
Axes of the slice: x: 4, y: 4, z: 8 (z_hi: 2, z_lo: 4; z = z_hi * 4 + z_lo), core: 2. Of those that a mesh axis runs over, the one named last changes fastest.
Arguments:
- embeddings: bfloat16 [32768, 768], P('rows'), may hold values from -40 to 40
- centroids: bfloat16 [4096, 768], P('cent'), may hold values from -6 to 6
- codebooks: float32 [96, 8, 256], replicated, may hold values from -6 to 6
Outputs:
- new_centroids: float32 [4096, 768], P('cent')
- new_codebooks: float32 [96, 8, 256], replicated
The draws below stay inside these ranges and needn't reach their ends.
All inputs are finite; a program needn't handle non-finite values.
Results may differ from the reference program's by a relative error of at most 0.001.
The reference program's roundings to bfloat16 on the way (of `wb`) count: a program that leaves them out, or rounds other values in their place, can miss the bound.
Values sent between devices are 32-bit elements; how exact they have to be, the bound alone decides.
No kernel may reach another device: no remote copies, remote signals or barrier semaphores. Data moves between devices by JAX's collectives and lax.ppermute only.
A program may use at most 64 MiB of HBM per device.

```python
import math
import jax
import jax.numpy as jnp
from jax import lax

D = 768
K = 4096
M = 96
KS = 256
R_DEV = 1024
DSUB = 8
N = 32768


def shared_centroids(key):
    return jnp.clip(jax.random.normal(key, (K, D), jnp.float32), -6.0, 6.0)


def draw_centroids(key, part):
    base = shared_centroids(key)
    return base.astype(jnp.bfloat16)


def draw_embeddings(key, part):
    key = jax.random.fold_in(key, 23)
    first_key = jax.random.fold_in(key, 0)
    values = jnp.clip(jax.random.normal(first_key, (N, D), jnp.float32), -6.0, 6.0)
    return values.astype(jnp.bfloat16)


def gaussian(stream_key, extent, spread, reach, dtype=jnp.bfloat16):
    result = spread * jax.random.normal(stream_key, extent, jnp.float32)
    return jnp.clip(result, min=-reach, max=reach).astype(dtype)


def setup_inputs(seed: int = 0) -> dict:
    key_list = jax.random.split(jax.random.key(seed), 4)
    embeddings = draw_embeddings(jax.random.fold_in(key_list[3], 71), 0)
    centroids = draw_centroids(jax.random.fold_in(key_list[3], 71), 0)
    codebooks = gaussian(key_list[2], (M, DSUB, KS), 1.0, 6.0, jnp.float32)
    return dict(embeddings=embeddings, centroids=centroids, codebooks=codebooks)


def codebook_sums(resid, codebooks):
    count = resid.shape[0]
    groups = codebooks.shape[0] // 8
    width = codebooks.shape[1]
    parts = resid.reshape(count, groups, 8, width).transpose(1, 0, 2, 3)
    books = codebooks.reshape(groups, 8, width, codebooks.shape[2])

    def one_group(pair):
        piece, book = pair
        dots = jnp.einsum('rmd,mdk->rmk', piece, book, precision=lax.Precision.HIGHEST)
        logits = dots - 0.5 * lax.optimization_barrier(jnp.sum(book * book, axis=1))[None]
        weights = jax.nn.softmax(logits, axis=-1)
        sums = jnp.einsum('rmk,rmd->mdk', weights, piece, precision=lax.Precision.HIGHEST)
        return (sums, lax.optimization_barrier(jnp.sum(weights, axis=0)))
    sums, counts = lax.map(one_group, (parts, books))
    return (sums.reshape(codebooks.shape), counts.reshape(codebooks.shape[0], codebooks.shape[2]))

def reference(embeddings, centroids, codebooks):
    cent_f = centroids.astype(jnp.float32)
    sq_norms = lax.optimization_barrier(jnp.sum(cent_f * cent_f, axis=1))
    blocks = embeddings.reshape(-1, R_DEV, D)

    def step(carry, block):
        mass, counts, book_sums, book_counts = carry
        cross = lax.dot_general(block, centroids, (((1,), (1,)), ((), ())), preferred_element_type=jnp.float32)
        logits = 3.0 * (cross - 0.5 * sq_norms[None, :]) / math.sqrt(D)
        weights = jax.nn.softmax(logits, axis=1)
        wb = weights.astype(jnp.bfloat16)
        mass = mass + lax.dot_general(wb, block, (((0,), (0,)), ((), ())), preferred_element_type=jnp.float32)
        counts = counts + lax.optimization_barrier(jnp.sum(weights, axis=0))
        resid = block.astype(jnp.float32) - jnp.dot(wb, centroids, preferred_element_type=jnp.float32)
        sums, tallies = codebook_sums(resid, codebooks)
        return ((mass, counts, book_sums + sums, book_counts + tallies), None)
    start = (jnp.zeros((K, D), jnp.float32), jnp.zeros((K,), jnp.float32), jnp.zeros(codebooks.shape, jnp.float32), jnp.zeros((M, KS), jnp.float32))
    (mass, counts, book_sums, book_counts), _ = lax.scan(step, start, blocks)
    new_centroids = (mass + cent_f) / (counts[:, None] + 1.0)
    new_codebooks = (book_sums + codebooks) / (book_counts[:, None, :] + 1.0)
    return (new_centroids, new_codebooks)
```

```python
import itertools
import math

import jax
import jax.numpy as jnp
from jax import lax
from jax.experimental import pallas as pl
from jax.experimental.pallas import tpu as pltpu
from jax.sharding import PartitionSpec as P

NX, NY, NZL, NZH, NC = 4, 4, 4, 2, 2
BOTH = ("rows", "cent")
F32, BF16 = jnp.float32, jnp.bfloat16


def flat(x, y, zl, zh, c):
    return ((x * NZL + zl) * NC + c) * (NY * NZH) + (y * NZH + zh)


def hop(value, move):
    pairs = []
    for place in itertools.product(range(NX), range(NY), range(NZL), range(NZH), range(NC)):
        pairs.append((flat(*place), flat(*move(*place))))
    return lax.ppermute(value, BOTH, pairs)


def along_x(k):
    return lambda x, y, zl, zh, c: ((x + k) % NX, y, zl, zh, c)


def along_y(k):
    return lambda x, y, zl, zh, c: (x, (y + k) % NY, zl, zh, c)


def along_zl(k):
    return lambda x, y, zl, zh, c: (x, y, zl ^ k, zh, c)


def other_zh(x, y, zl, zh, c):
    return (x, y, zl, 1 - zh, c)


def other_core(x, y, zl, zh, c):
    return (x, y, zl, zh, 1 - c)


def call(kernel, out, args, smem=0, scratch=(), flops=0, limit=48):
    nbytes = sum(a.size * a.dtype.itemsize for a in args)
    specs = [pl.BlockSpec(memory_space=pltpu.SMEM)] * smem
    specs += [pl.BlockSpec(memory_space=pltpu.VMEM)] * (len(args) - smem)
    return pl.pallas_call(
        kernel,
        out_shape=out,
        in_specs=specs,
        out_specs=jax.tree.map(lambda _: pl.BlockSpec(memory_space=pltpu.VMEM), out),
        scratch_shapes=list(scratch),
        compiler_params=pltpu.CompilerParams(vmem_limit_bytes=limit * 1024 * 1024),
        cost_estimate=pl.CostEstimate(flops=flops, bytes_accessed=2 * nbytes, transcendentals=0),
    )(*args)


def shape(dims, dtype=F32):
    return jax.ShapeDtypeStruct(dims, dtype)


def dot(a, b, ca, cb):
    return lax.dot_general(a, b, (((ca,), (cb,)), ((), ())), preferred_element_type=F32)


def logits_kernel(emb_ref, cent_ref, p_ref, stat_ref):
    rows, width = emb_ref.shape
    cent = cent_ref[...]
    cent_f = cent.astype(F32)
    half_sq = 0.5 * jnp.sum(cent_f * cent_f, axis=1, keepdims=True)
    step = 256
    tops, sums = [], []
    for start in range(0, rows, step):
        cross = dot(cent, emb_ref[start : start + step, :], 1, 1)
        logits = (cross - half_sq) * (3.0 / math.sqrt(width))
        top = jnp.max(logits, axis=0, keepdims=True)
        p = jnp.exp(logits - top)
        p_ref[:, start : start + step] = p
        tops.append(top)
        sums.append(jnp.sum(p, axis=0, keepdims=True))
    block = jnp.concatenate(
        [
            jnp.concatenate(tops, axis=1).reshape(rows // 128, 128),
            jnp.concatenate(sums, axis=1).reshape(rows // 128, 128),
        ],
        axis=0,
    )
    for i in range(stat_ref.shape[0]):
        stat_ref[i] = block


def weights_kernel(place_ref, p_ref, mine_ref, stat_ref, cent_t_ref, wb_ref, count_ref, *out_refs):
    y, zh = place_ref[1], place_ref[3]
    half = stat_ref.shape[1] // 2
    tops = stat_ref[:, :half, :]
    top = jnp.max(tops, axis=0)
    total = jnp.sum(stat_ref[:, half:, :] * jnp.exp(tops - top[None]), axis=0)
    scale = jnp.exp(mine_ref[0, :half, :] - top) / total
    scale = scale.reshape(1, p_ref.shape[1])
    w = p_ref[...] * scale
    count_ref[...] = jnp.broadcast_to(jnp.sum(w, axis=1, keepdims=True), count_ref.shape)
    wb_ref[...] = w.astype(BF16)
    share = out_refs[0].shape[0]
    for part in range(2):
        for k in range(NY):
            side = (1 - zh) if part == 0 else zh
            start = ((y + k) % NY) * (NZH * share) + side * share
            piece = cent_t_ref[pl.ds(pl.multiple_of(start, 16), share), :]
            out_refs[part * NY + k][...] = dot(piece, wb_ref[...], 1, 0)


def mass_kernel(place_ref, wb_ref, count_ref, emb_ref, keep_ref, send_ref):
    c = place_ref[4]
    half, width = keep_ref.shape[0], emb_ref.shape[1]
    for ref, side in ((keep_ref, c), (send_ref, 1 - c)):
        here = pl.ds(pl.multiple_of(side * half, 16), half)
        ref[:, :width] = dot(wb_ref[here, :], emb_ref[...], 1, 0)
        ref[:, width:] = count_ref[here, :]


def pieces(v):
    hi = v.astype(BF16).astype(F32)
    rest = v - hi
    mid = rest.astype(BF16).astype(F32)
    return hi, mid, rest - mid


def codebook_kernel(emb_t_ref, a_ref, b_ref, c_ref, d_ref, e_ref, books_ref, out_ref):
    subspaces, depth, codes = books_ref.shape
    rows = emb_t_ref.shape[1]
    ones = jnp.where(lax.broadcasted_iota(jnp.int32, (2 * depth, rows), 0) < 3, 1.0, 0.0)
    for m in range(subspaces):
        at = slice(m * depth, (m + 1) * depth)
        recon = a_ref[at, :] + b_ref[at, :] + c_ref[at, :] + d_ref[at, :] + e_ref[at, :]
        r = emb_t_ref[at, :] - recon
        r0, r1, r2 = pieces(r)
        book = books_ref[m]
        k0, k1, k2 = pieces(book)
        s0, s1, s2 = pieces(-0.5 * jnp.sum(book * book, axis=0, keepdims=True))
        zero = jnp.zeros((2 * depth - 3, codes), F32)
        left = jnp.concatenate([k0, k0, k1, k0, k2, k1, s0, s1, s2, zero], axis=0).astype(BF16)
        right = jnp.concatenate([r0, r1, r0, r2, r0, r1, ones], axis=0).astype(BF16)
        logits = dot(left, right, 0, 0)
        p = jnp.exp(logits - jnp.max(logits, axis=0, keepdims=True))
        inv = 1.0 / jnp.sum(p, axis=0, keepdims=True)
        q0, q1, q2 = pieces(r * inv)
        i0, i1, i2 = pieces(jnp.broadcast_to(inv, (depth, rows)))
        scaled = jnp.concatenate([q0, q1, q2, i0, i1, i2], axis=0).astype(BF16)
        p_hi = p.astype(BF16)
        p_lo = (p - p_hi.astype(F32)).astype(BF16)
        high = dot(scaled, p_hi, 1, 1)
        low = dot(scaled, p_lo, 1, 1)
        mass = high[:depth] + (high[depth : 2 * depth] + (high[2 * depth : 3 * depth] + low[:depth]))
        mass = mass + low[depth : 2 * depth]
        o = 3 * depth
        count = high[o : o + 1] + (high[o + depth : o + depth + 1] + low[o : o + 1])
        count = count + high[o + 2 * depth : o + 2 * depth + 1] + low[o + depth : o + depth + 1]
        for d in range(depth):
            owner, slot = divmod(m * depth + d, 3)
            core, xz = divmod(owner, NX * NZL)
            row = xz * NC + core
            out_ref[row, slot : slot + 1, :] = mass[d : d + 1]
            out_ref[row, slot + 3 : slot + 4, :] = count


def update_kernel(parts_ref, book_ref, out_ref):
    total = jnp.sum(parts_ref[...], axis=0)
    new = (total[:3] + book_ref[:3]) / (total[3:6] + 1.0)
    tile = jnp.concatenate([new[:, :128], new[:, 128:], jnp.zeros((2, 128), F32)], axis=0)
    for i in range(out_ref.shape[0]):
        out_ref[i] = tile


def books_kernel(place_ref, mine_ref, theirs_ref, out_ref):
    core = place_ref[4]
    count = mine_ref.shape[0]
    group = NX * NZL

    def place(first_ref, second_ref):
        for side, ref in ((0, first_ref), (1, second_ref)):
            for i in range(count):
                cent, xz = divmod(i, group)
                row = (cent * NC + side) * group * 3 + xz * 3
                out_ref[row : row + 3, :128] = ref[i, :3, :]
                out_ref[row : row + 3, 128:] = ref[i, 3:6, :]

    @pl.when(core == 0)
    def _():
        place(mine_ref, theirs_ref)

    @pl.when(core == 1)
    def _():
        place(theirs_ref, mine_ref)


def centroids_kernel(place_ref, mine_ref, theirs_ref, out_ref):
    x, zl, c = place_ref[0], place_ref[2], place_ref[4]
    rows = mine_ref.shape[0] // (NX * NZL)
    for ref, side in ((mine_ref, c), (theirs_ref, 1 - c)):
        for kx in range(NX):
            for kz in range(NZL):
                spot = (side * NX + (x + NX - kx) % NX) * NZL + lax.bitwise_xor(zl, kz)
                at = (kx * NZL + kz) * rows
                out_ref[pl.ds(pl.multiple_of(spot * rows, 8), rows), :] = ref[at : at + rows, :]


def body(embeddings, centroids, codebooks):
    rows_here, width = embeddings.shape
    held = centroids.shape[0]
    subspaces, depth, codes = codebooks.shape
    row_at = lax.axis_index("rows")
    cent_at = lax.axis_index("cent")
    x, zl, c = row_at // (NZL * NC), (row_at // NC) % NZL, row_at % NC
    y, zh = cent_at // NZH, cent_at % NZH
    place = jnp.stack([x, y, zl, zh, c]).astype(jnp.int32)
    cents = NY * NZH
    share = width // cents

    p, stat = call(
        logits_kernel,
        (shape((held, rows_here)), shape((cents, 2 * rows_here // 128, 128))),
        (embeddings, centroids),
        flops=2 * rows_here * held * width,
    )
    stats = lax.all_to_all(stat, "cent", 0, 0, tiled=True)
    outs = call(
        weights_kernel,
        (shape((held, rows_here), BF16), shape((held, 128))) + (shape((share, rows_here)),) * 8,
        (place, p, stat, stats, centroids.T),
        smem=1,
        flops=2 * rows_here * held * width,
    )
    wb, counts, theirs, mine = outs[0], outs[1], outs[2:6], outs[6:10]
    steps = (1, -1, 2)
    got = [hop(theirs[k % NY], along_y(k)) for k in steps]
    got_mine = [hop(mine[k % NY], along_y(k)) for k in steps]
    peer = hop(theirs[0] + got[0] + got[1] + got[2], other_zh)

    keep, send = call(
        mass_kernel,
        (shape((held // 2, width + 128)),) * 2,
        (place, wb, counts, embeddings),
        smem=1,
        flops=2 * rows_here * held * width,
    )
    mass = keep + hop(send, other_core)
    groups = [
        [(xx * NZL + zz) * NC + cc for xx in range(NX) for zz in range(NZL)] for cc in range(NC)
    ]
    peers = NX * NZL
    piece_rows = held // (2 * peers)
    parts = lax.all_to_all(
        mass.reshape(peers, piece_rows, width + 128), "rows", 0, 0, tiled=True, axis_index_groups=groups
    )
    total = jnp.sum(parts, axis=0)
    first = c * (held // 2) + (x * NZL + zl) * piece_rows
    old = lax.dynamic_slice_in_dim(centroids, first, piece_rows, 0).astype(F32)
    new = (total[:, :width] + old) / (total[:, width : width + 1] + 1.0)

    emb_t = lax.dynamic_slice_in_dim(embeddings, cent_at * share, share, 1).T.astype(F32)
    per = subspaces // cents
    my_books = lax.dynamic_slice_in_dim(codebooks, cent_at * per, per, 0)
    sums = call(
        codebook_kernel,
        shape((NX * NZL * NC, 8, codes)),
        (emb_t, mine[0], *got_mine, peer, my_books),
        flops=4 * rows_here * per * codes * 64,
    )
    new_z = jnp.concatenate([new] + [hop(new, along_zl(k)) for k in (1, 2, 3)], axis=0)
    owner = c * peers + x * NZL + zl
    flat_books = jnp.pad(codebooks.reshape(subspaces * depth, codes), ((0, 8), (0, 0)))
    my_rows = lax.dynamic_slice_in_dim(flat_books, (cent_at * NC * peers + owner) * 3, 8, 0)
    all_parts = lax.all_to_all(sums, "rows", 0, 0, tiled=True)
    same_core = [
        [flat(xx, yy, zz, hh, cc) for yy in range(NY) for hh in range(NZH) for xx in range(NX) for zz in range(NZL)]
        for cc in range(NC)
    ]
    tile = call(update_kernel, shape((cents * peers, 8, 128)), (all_parts, my_rows))
    new_x = jnp.concatenate([new_z] + [hop(new_z, along_x(k)) for k in (1, 2, 3)], axis=0)
    new_other = hop(new_x, other_core)
    new_centroids = call(
        centroids_kernel, shape((held, width)), (place, new_x, new_other), smem=1
    )
    tiles = lax.all_to_all(tile, BOTH, 0, 0, tiled=True, axis_index_groups=same_core)
    tiles_other = hop(tiles, other_core)
    new_books = call(
        books_kernel, shape((subspaces * depth, codes)), (place, tiles, tiles_other), smem=1
    )
    return (new_centroids, new_books.reshape(codebooks.shape))


def solution(mesh):
    in_specs = (P("rows", None), P("cent", None), P())
    out_specs = (P("cent", None), P())
    return jax.shard_map(body, mesh=mesh, in_specs=in_specs, out_specs=out_specs, check_vma=False)
```

```python
import itertools
import math

import jax
import jax.numpy as jnp
from jax import lax
from jax.experimental import pallas as pl
from jax.experimental.pallas import tpu as pltpu
from jax.sharding import PartitionSpec as P

NX, NY, NZL, NZH, NC = 4, 4, 4, 2, 2
BOTH = ("rows", "cent")
F32, BF16 = jnp.float32, jnp.bfloat16


def flat(x, y, zl, zh, c):
    return ((x * NZL + zl) * NC + c) * (NY * NZH) + (y * NZH + zh)


def hop(value, move):
    pairs = []
    for place in itertools.product(range(NX), range(NY), range(NZL), range(NZH), range(NC)):
        pairs.append((flat(*place), flat(*move(*place))))
    return lax.ppermute(value, BOTH, pairs)


def along_x(k):
    return lambda x, y, zl, zh, c: (x ^ k, y, zl, zh, c)


def along_y(k):
    return lambda x, y, zl, zh, c: (x, (y + k) % NY, zl, zh, c)


def along_zl(k):
    return lambda x, y, zl, zh, c: (x, y, zl ^ k, zh, c)


def other_zh(x, y, zl, zh, c):
    return (x, y, zl, 1 - zh, c)


def other_core(x, y, zl, zh, c):
    return (x, y, zl, zh, 1 - c)


def call(kernel, out, args, smem=0, scratch=(), flops=0, limit=12, hbm_in=0):
    nbytes = sum(a.size * a.dtype.itemsize for a in args)
    specs = [pl.BlockSpec(memory_space=pltpu.SMEM)] * smem
    specs += [pl.BlockSpec(memory_space=pl.ANY)] * hbm_in
    specs += [pl.BlockSpec(memory_space=pltpu.VMEM)] * (len(args) - smem - hbm_in)
    return pl.pallas_call(
        kernel,
        out_shape=out,
        in_specs=specs,
        out_specs=jax.tree.map(lambda _: pl.BlockSpec(memory_space=pltpu.VMEM), out),
        scratch_shapes=list(scratch),
        compiler_params=pltpu.CompilerParams(vmem_limit_bytes=limit * 1024 * 1024),
        cost_estimate=pl.CostEstimate(flops=flops, bytes_accessed=2 * nbytes, transcendentals=0),
    )(*args)


def shape(dims, dtype=F32):
    return jax.ShapeDtypeStruct(dims, dtype)


def dot(a, b, ca, cb):
    return lax.dot_general(a, b, (((ca,), (cb,)), ((), ())), preferred_element_type=F32)


def relative_blocks(place_ref):
    x, zl, c = place_ref[0], place_ref[2], place_ref[4]
    spots = []
    for kc, kx, kz in itertools.product(range(NC), range(NX), range(NZL)):
        spot = (lax.bitwise_xor(c, kc) * NX + lax.bitwise_xor(x, kx)) * NZL + lax.bitwise_xor(zl, kz)
        spots.append(spot)
    return spots


def logits_kernel(place_ref, emb_ref, cent_ref, p_ref, stat_ref, held_ref, emb_buf, sems):
    rows, width = emb_ref.shape
    step = 256
    spots = relative_blocks(place_ref)
    size = cent_ref.shape[0] // len(spots)
    copies = []
    for i, spot in enumerate(spots):
        source = cent_ref.at[pl.ds(pl.multiple_of(spot * size, 16), size), :]
        copies.append(pltpu.make_async_copy(source, held_ref.at[i * size : (i + 1) * size, :], sems.at[i]))
    for i in range(rows // step):
        at = slice(i * step, (i + 1) * step)
        copies.append(pltpu.make_async_copy(emb_ref.at[at, :], emb_buf.at[at, :], sems.at[len(spots) + i]))
    for copy in copies:
        copy.start()
    for copy in copies[: len(spots)]:
        copy.wait()
    cent = held_ref[...]
    cent_f = cent.astype(F32)
    half_sq = 0.5 * jnp.sum(cent_f * cent_f, axis=1, keepdims=True)
    tops, sums = [], []
    for i in range(rows // step):
        start = i * step
        copies[len(spots) + i].wait()
        cross = dot(cent, emb_buf[start : start + step, :], 1, 1)
        logits = (cross - half_sq) * (3.0 / math.sqrt(width))
        top = jnp.max(logits, axis=0, keepdims=True)
        p = jnp.exp(logits - top)
        p_ref[:, start : start + step] = p
        tops.append(top)
        sums.append(jnp.sum(p, axis=0, keepdims=True))
    block = jnp.concatenate(
        [
            jnp.concatenate(tops, axis=1).reshape(rows // 128, 128),
            jnp.concatenate(sums, axis=1).reshape(rows // 128, 128),
        ],
        axis=0,
    )
    for i in range(stat_ref.shape[0]):
        stat_ref[i] = block


def weights_kernel(place_ref, p_ref, mine_ref, stat_ref, cent_t_ref, wb_ref, count_ref, *out_refs):
    y, zh = place_ref[1], place_ref[3]
    half = stat_ref.shape[1] // 2
    tops = stat_ref[:, :half, :]
    top = jnp.max(tops, axis=0)
    total = jnp.sum(stat_ref[:, half:, :] * jnp.exp(tops - top[None]), axis=0)
    scale = jnp.exp(mine_ref[0, :half, :] - top) / total
    scale = scale.reshape(1, p_ref.shape[1])
    w = p_ref[...] * scale
    count_ref[...] = jnp.broadcast_to(jnp.sum(w, axis=1, keepdims=True), count_ref.shape)
    wb_ref[...] = w.astype(BF16)
    share = out_refs[0].shape[0]
    for part in range(2):
        for k in range(NY):
            side = (1 - zh) if part == 0 else zh
            start = ((y + k) % NY) * (NZH * share) + side * share
            piece = cent_t_ref[pl.ds(pl.multiple_of(start, 16), share), :]
            out_refs[part * NY + k][...] = dot(piece, wb_ref[...], 1, 0)


def mass_kernel(place_ref, wb_ref, count_ref, emb_ref, keep_ref, send_ref, emb_t_ref, turned_ref):
    half, width = keep_ref.shape[0], emb_ref.shape[1]
    for ref, start in ((send_ref, half), (keep_ref, 0)):
        ref[:, :width] = dot(wb_ref[start : start + half, :], emb_ref[...], 1, 0)
        ref[:, width:] = count_ref[start : start + half, :]
    share = emb_t_ref.shape[0]
    turned_ref[...] = emb_ref[...].T
    first = (place_ref[1] * NZH + place_ref[3]) * share
    emb_t_ref[...] = turned_ref[pl.ds(pl.multiple_of(first, 16), share), :].astype(F32)


def halve_kernel(mine_ref, got_ref, keep_ref, send_ref):
    half = keep_ref.shape[0]
    keep_ref[...] = mine_ref[:half, :] + got_ref[:half, :]
    send_ref[...] = mine_ref[half:, :] + got_ref[half:, :]


def centroid_kernel(mine_ref, got_ref, old_ref, out_ref):
    rows, width = out_ref.shape
    total = mine_ref[...] + got_ref[...]
    old = old_ref[:rows, :].astype(F32)
    out_ref[...] = (total[:, :width] + old) / (total[:, width : width + 1] + 1.0)


def add_kernel(a_ref, b_ref, c_ref, d_ref, out_ref):
    out_ref[...] = (a_ref[...] + b_ref[...]) + (c_ref[...] + d_ref[...])


def pieces(v):
    hi = v.astype(BF16).astype(F32)
    rest = v - hi
    mid = rest.astype(BF16).astype(F32)
    return hi, mid, rest - mid


def codebook_kernel(
    place_ref, all_books_ref, emb_t_ref, a_ref, b_ref, c_ref, d_ref, e_ref, out_ref, books_ref, sem
):
    subspaces, depth, codes = books_ref.shape
    first = (place_ref[1] * NZH + place_ref[3]) * subspaces
    copy = pltpu.make_async_copy(all_books_ref.at[pl.ds(first, subspaces)], books_ref, sem)
    copy.start()
    copy.wait()
    rows = emb_t_ref.shape[1]
    ones = jnp.where(lax.broadcasted_iota(jnp.int32, (2 * depth, rows), 0) < 3, 1.0, 0.0)
    for m in range(subspaces):
        at = slice(m * depth, (m + 1) * depth)
        recon = a_ref[at, :] + b_ref[at, :] + c_ref[at, :] + d_ref[at, :] + e_ref[at, :]
        r = emb_t_ref[at, :] - recon
        r0, r1, r2 = pieces(r)
        book = books_ref[m]
        k0, k1, k2 = pieces(book)
        s0, s1, s2 = pieces(-0.5 * jnp.sum(book * book, axis=0, keepdims=True))
        zero = jnp.zeros((2 * depth - 3, codes), F32)
        left = jnp.concatenate([k0, k0, k1, k0, k2, k1, s0, s1, s2, zero], axis=0).astype(BF16)
        right = jnp.concatenate([r0, r1, r0, r2, r0, r1, ones], axis=0).astype(BF16)
        logits = dot(left, right, 0, 0)
        p = jnp.exp(logits - jnp.max(logits, axis=0, keepdims=True))
        inv = 1.0 / jnp.sum(p, axis=0, keepdims=True)
        q0, q1, q2 = pieces(r * inv)
        i0, i1, i2 = pieces(jnp.broadcast_to(inv, (depth, rows)))
        scaled = jnp.concatenate([q0, q1, q2, i0, i1, i2], axis=0).astype(BF16)
        p_hi = p.astype(BF16)
        p_lo = (p - p_hi.astype(F32)).astype(BF16)
        high = dot(scaled, p_hi, 1, 1)
        low = dot(scaled, p_lo, 1, 1)
        mass = high[:depth] + (high[depth : 2 * depth] + (high[2 * depth : 3 * depth] + low[:depth]))
        mass = mass + low[depth : 2 * depth]
        o = 3 * depth
        count = high[o : o + 1] + (high[o + depth : o + depth + 1] + low[o : o + 1])
        count = count + high[o + 2 * depth : o + 2 * depth + 1] + low[o + depth : o + depth + 1]
        for d in range(depth):
            owner, slot = divmod(m * depth + d, 3)
            core, xz = divmod(owner, NX * NZL)
            row = xz * NC + core
            out_ref[row, slot : slot + 1, :] = mass[d : d + 1]
            out_ref[row, slot + 3 : slot + 4, :] = count


def update_kernel(place_ref, all_books_ref, parts_ref, out_ref, books_ref, sem):
    x, y, zl, zh, c = (place_ref[i] for i in range(5))
    share = books_ref.shape[0]
    first = pl.multiple_of((y * NZH + zh) * share, 8)
    copy = pltpu.make_async_copy(all_books_ref.at[pl.ds(first, share), :], books_ref, sem)
    copy.start()
    total = jnp.sum(parts_ref[...], axis=0)
    copy.wait()
    row = ((c * NX + x) * NZL + zl) * 3
    old = jnp.concatenate([books_ref[pl.ds(row + i, 1), :] for i in range(3)], axis=0)
    new = (total[:3] + old) / (total[3:6] + 1.0)
    tile = jnp.concatenate([new[:, :128], new[:, 128:], jnp.zeros((2, 128), F32)], axis=0)
    for i in range(out_ref.shape[0]):
        out_ref[i] = tile


def books_kernel(place_ref, mine_ref, theirs_ref, out_ref):
    core = place_ref[4]
    count = mine_ref.shape[0]
    group = NX * NZL

    def place(first_ref, second_ref):
        for side, ref in ((0, first_ref), (1, second_ref)):
            for i in range(count):
                cent, xz = divmod(i, group)
                row = (cent * NC + side) * group * 3 + xz * 3
                out_ref[row : row + 3, :128] = ref[i, :3, :]
                out_ref[row : row + 3, 128:] = ref[i, 3:6, :]

    @pl.when(core == 0)
    def _():
        place(mine_ref, theirs_ref)

    @pl.when(core == 1)
    def _():
        place(theirs_ref, mine_ref)


def centroids_kernel(place_ref, mine_ref, theirs_ref, out_ref):
    spots = relative_blocks(place_ref)
    half = len(spots) // 2
    size = mine_ref.shape[0] // half
    for i, spot in enumerate(spots):
        ref = mine_ref if i < half else theirs_ref
        at = (i % half) * size
        out_ref[pl.ds(pl.multiple_of(spot * size, 8), size), :] = ref[at : at + size, :]


def body(embeddings, centroids, codebooks):
    rows_here, width = embeddings.shape
    held = centroids.shape[0]
    subspaces, depth, codes = codebooks.shape
    row_at = lax.axis_index("rows")
    cent_at = lax.axis_index("cent")
    x, zl, c = row_at // (NZL * NC), (row_at // NC) % NZL, row_at % NC
    y, zh = cent_at // NZH, cent_at % NZH
    place = jnp.stack([x, y, zl, zh, c]).astype(jnp.int32)
    cents = NY * NZH
    share = width // cents

    p, stat, ordered = call(
        logits_kernel,
        (
            shape((held, rows_here)),
            shape((cents, 2 * rows_here // 128, 128)),
            shape((held, width), BF16),
        ),
        (place, embeddings, centroids),
        smem=1,
        hbm_in=2,
        scratch=(pltpu.VMEM((rows_here, width), BF16), pltpu.SemaphoreType.DMA((64,))),
        limit=60,
        flops=2 * rows_here * held * width,
    )
    stats = lax.all_to_all(stat, "cent", 0, 0, tiled=True)
    outs = call(
        weights_kernel,
        (shape((held, rows_here), BF16), shape((held, 128))) + (shape((share, rows_here)),) * 8,
        (place, p, stat, stats, ordered.T),
        smem=1,
        flops=2 * rows_here * held * width,
    )
    wb, counts, theirs, mine = outs[0], outs[1], outs[2:6], outs[6:10]
    steps = (1, -1, 2)
    got = [hop(theirs[k % NY], along_y(k)) for k in steps]
    got_mine = [hop(mine[k % NY], along_y(k)) for k in steps]
    peer = hop(call(add_kernel, shape((share, rows_here)), (theirs[0], *got)), other_zh)

    keep, send, emb_t = call(
        mass_kernel,
        (shape((held // 2, width + 128)),) * 2 + (shape((share, rows_here)),),
        (place, wb, counts, embeddings),
        smem=1,
        scratch=(pltpu.VMEM((width, rows_here), BF16),),
        flops=2 * rows_here * held * width,
    )
    for move in (other_core, along_x(2), along_x(1), along_zl(2)):
        half = keep.shape[0] // 2
        keep, send = call(
            halve_kernel, (shape((half, width + 128)),) * 2, (keep, hop(send, move)), limit=4
        )
    new = call(
        centroid_kernel, shape((half, width)), (keep, hop(send, along_zl(1)), ordered), limit=4
    )
    peers = NX * NZL

    per = subspaces // cents
    sums = call(
        codebook_kernel,
        shape((NX * NZL * NC, 8, codes)),
        (place, codebooks, emb_t, mine[0], *got_mine, peer),
        smem=1,
        hbm_in=1,
        scratch=(pltpu.VMEM((per, depth, codes), F32), pltpu.SemaphoreType.DMA),
        flops=64 * rows_here * per * codes * 64,
    )
    new_z = jnp.concatenate([new] + [hop(new, along_zl(k)) for k in (1, 2, 3)], axis=0)
    all_parts = lax.all_to_all(sums, "rows", 0, 0, tiled=True)
    same_core = [
        [flat(xx, yy, zz, hh, cc) for yy in range(NY) for hh in range(NZH) for xx in range(NX) for zz in range(NZL)]
        for cc in range(NC)
    ]
    tile = call(
        update_kernel,
        shape((cents * peers, 8, 128)),
        (place, codebooks.reshape(subspaces * depth, codes), all_parts),
        smem=1,
        hbm_in=1,
        scratch=(pltpu.VMEM((share, codes), F32), pltpu.SemaphoreType.DMA),
    )
    new_x = jnp.concatenate([new_z] + [hop(new_z, along_x(k)) for k in (1, 2, 3)], axis=0)
    new_other = hop(new_x, other_core)
    new_centroids = call(
        centroids_kernel, shape((held, width)), (place, new_x, new_other), smem=1
    )
    tiles = lax.all_to_all(tile, BOTH, 0, 0, tiled=True, axis_index_groups=same_core)
    tiles_other = hop(tiles, other_core)
    new_books = call(
        books_kernel, shape((subspaces * depth, codes)), (place, tiles, tiles_other), smem=1
    )
    return (new_centroids, new_books.reshape(codebooks.shape))


def solution(mesh):
    in_specs = (P("rows", None), P("cent", None), P())
    out_specs = (P("cent", None), P())
    return jax.shard_map(body, mesh=mesh, in_specs=in_specs, out_specs=out_specs, check_vma=False)
```

```python
import itertools
import math

import jax
import jax.numpy as jnp
from jax import lax
from jax.experimental import pallas as pl
from jax.experimental.pallas import tpu as pltpu
from jax.sharding import PartitionSpec as P

NX, NY, NZL, NZH, NC = 4, 4, 4, 2, 2
BOTH = ("rows", "cent")
F32, BF16 = jnp.float32, jnp.bfloat16


def flat(x, y, zl, zh, c):
    return ((x * NZL + zl) * NC + c) * (NY * NZH) + (y * NZH + zh)


def hop(value, move):
    pairs = []
    for place in itertools.product(range(NX), range(NY), range(NZL), range(NZH), range(NC)):
        pairs.append((flat(*place), flat(*move(*place))))
    return lax.ppermute(value, BOTH, pairs)


def along_x(k):
    return lambda x, y, zl, zh, c: (x ^ k, y, zl, zh, c)


def along_y(k):
    return lambda x, y, zl, zh, c: (x, (y + k) % NY, zl, zh, c)


def along_zl(k):
    return lambda x, y, zl, zh, c: (x, y, zl ^ k, zh, c)


def other_zh(x, y, zl, zh, c):
    return (x, y, zl, 1 - zh, c)


def other_core(x, y, zl, zh, c):
    return (x, y, zl, zh, 1 - c)


def call(kernel, out, args, smem=0, scratch=(), flops=0, limit=12, hbm_in=0):
    nbytes = sum(a.size * a.dtype.itemsize for a in args)
    specs = [pl.BlockSpec(memory_space=pltpu.SMEM)] * smem
    specs += [pl.BlockSpec(memory_space=pl.ANY)] * hbm_in
    specs += [pl.BlockSpec(memory_space=pltpu.VMEM)] * (len(args) - smem - hbm_in)
    return pl.pallas_call(
        kernel,
        out_shape=out,
        in_specs=specs,
        out_specs=jax.tree.map(lambda _: pl.BlockSpec(memory_space=pltpu.VMEM), out),
        scratch_shapes=list(scratch),
        compiler_params=pltpu.CompilerParams(vmem_limit_bytes=limit * 1024 * 1024),
        cost_estimate=pl.CostEstimate(flops=flops, bytes_accessed=2 * nbytes, transcendentals=0),
    )(*args)


def shape(dims, dtype=F32):
    return jax.ShapeDtypeStruct(dims, dtype)


def dot(a, b, ca, cb):
    return lax.dot_general(a, b, (((ca,), (cb,)), ((), ())), preferred_element_type=F32)


def relative_blocks(place_ref):
    x, zl, c = place_ref[0], place_ref[2], place_ref[4]
    spots = []
    for kc, kx, kz in itertools.product(range(NC), range(NX), range(NZL)):
        spot = (lax.bitwise_xor(c, kc) * NX + lax.bitwise_xor(x, kx)) * NZL + lax.bitwise_xor(zl, kz)
        spots.append(spot)
    return spots


def logits_kernel(place_ref, emb_ref, cent_ref, p_ref, stat_ref, cent_t_ref, old_ref, held_ref):
    rows, width = emb_ref.shape
    step = 256
    spots = relative_blocks(place_ref)
    size = cent_ref.shape[0] // len(spots)
    for i, spot in enumerate(spots):
        held_ref[i * size : (i + 1) * size, :] = cent_ref[pl.ds(pl.multiple_of(spot * size, 16), size), :]
    cent = held_ref[...]
    cent_t_ref[...] = cent.T
    old_ref[...] = cent[:size, :].astype(F32)
    cent_f = cent.astype(F32)
    half_sq = 0.5 * jnp.sum(cent_f * cent_f, axis=1, keepdims=True)
    tops, sums = [], []
    for start in range(0, rows, step):
        cross = dot(cent, emb_ref[start : start + step, :], 1, 1)
        logits = (cross - half_sq) * (3.0 / math.sqrt(width))
        top = jnp.max(logits, axis=0, keepdims=True)
        p = jnp.exp(logits - top)
        p_ref[:, start : start + step] = p
        tops.append(top)
        sums.append(jnp.sum(p, axis=0, keepdims=True))
    block = jnp.concatenate(
        [
            jnp.concatenate(tops, axis=1).reshape(rows // 128, 128),
            jnp.concatenate(sums, axis=1).reshape(rows // 128, 128),
        ],
        axis=0,
    )
    for i in range(stat_ref.shape[0]):
        stat_ref[i] = block


def weights_kernel(place_ref, p_ref, mine_ref, stat_ref, cent_t_ref, wb_ref, count_ref, *out_refs):
    y, zh = place_ref[1], place_ref[3]
    half = stat_ref.shape[1] // 2
    tops = stat_ref[:, :half, :]
    top = jnp.max(tops, axis=0)
    total = jnp.sum(stat_ref[:, half:, :] * jnp.exp(tops - top[None]), axis=0)
    scale = jnp.exp(mine_ref[0, :half, :] - top) / total
    scale = scale.reshape(1, p_ref.shape[1])
    w = p_ref[...] * scale
    count_ref[...] = jnp.broadcast_to(jnp.sum(w, axis=1, keepdims=True), count_ref.shape)
    wb_ref[...] = w.astype(BF16)
    share = out_refs[0].shape[0]
    for part in range(2):
        for k in range(NY):
            side = (1 - zh) if part == 0 else zh
            start = ((y + k) % NY) * (NZH * share) + side * share
            piece = cent_t_ref[pl.ds(pl.multiple_of(start, 16), share), :]
            out_refs[part * NY + k][...] = dot(piece, wb_ref[...], 1, 0)


def mass_kernel(place_ref, wb_ref, count_ref, emb_ref, keep_ref, send_ref, emb_t_ref, turned_ref):
    half, width = keep_ref.shape[0], emb_ref.shape[1]
    for ref, start in ((send_ref, half), (keep_ref, 0)):
        ref[:, :width] = dot(wb_ref[start : start + half, :], emb_ref[...], 1, 0)
        ref[:, width:] = count_ref[start : start + half, :]
    share = emb_t_ref.shape[0]
    turned_ref[...] = emb_ref[...].T
    first = (place_ref[1] * NZH + place_ref[3]) * share
    emb_t_ref[...] = turned_ref[pl.ds(pl.multiple_of(first, 16), share), :].astype(F32)


def halve_kernel(mine_ref, got_ref, keep_ref, send_ref):
    half = keep_ref.shape[0]
    keep_ref[...] = mine_ref[:half, :] + got_ref[:half, :]
    send_ref[...] = mine_ref[half:, :] + got_ref[half:, :]


def centroid_kernel(mine_ref, got_ref, old_ref, out_ref):
    rows, width = out_ref.shape
    total = mine_ref[...] + got_ref[...]
    out_ref[...] = (total[:, :width] + old_ref[...]) / (total[:, width : width + 1] + 1.0)


def add_kernel(a_ref, b_ref, c_ref, d_ref, out_ref):
    out_ref[...] = (a_ref[...] + b_ref[...]) + (c_ref[...] + d_ref[...])


def pieces(v):
    hi = v.astype(BF16).astype(F32)
    rest = v - hi
    mid = rest.astype(BF16).astype(F32)
    return hi, mid, rest - mid


def codebook_kernel(
    place_ref, all_books_ref, emb_t_ref, a_ref, b_ref, c_ref, d_ref, e_ref, out_ref, books_ref, sem
):
    subspaces, depth, codes = books_ref.shape
    first = (place_ref[1] * NZH + place_ref[3]) * subspaces
    copy = pltpu.make_async_copy(all_books_ref.at[pl.ds(first, subspaces)], books_ref, sem)
    copy.start()
    copy.wait()
    rows = emb_t_ref.shape[1]
    ones = jnp.where(lax.broadcasted_iota(jnp.int32, (2 * depth, rows), 0) < 3, 1.0, 0.0)
    for m in range(subspaces):
        at = slice(m * depth, (m + 1) * depth)
        recon = a_ref[at, :] + b_ref[at, :] + c_ref[at, :] + d_ref[at, :] + e_ref[at, :]
        r = emb_t_ref[at, :] - recon
        r0, r1, r2 = pieces(r)
        book = books_ref[m]
        k0, k1, k2 = pieces(book)
        s0, s1, s2 = pieces(-0.5 * jnp.sum(book * book, axis=0, keepdims=True))
        zero = jnp.zeros((2 * depth - 3, codes), F32)
        left = jnp.concatenate([k0, k0, k1, k0, k2, k1, s0, s1, s2, zero], axis=0).astype(BF16)
        right = jnp.concatenate([r0, r1, r0, r2, r0, r1, ones], axis=0).astype(BF16)
        logits = dot(left, right, 0, 0)
        p = jnp.exp(logits - jnp.max(logits, axis=0, keepdims=True))
        inv = 1.0 / jnp.sum(p, axis=0, keepdims=True)
        q0, q1, q2 = pieces(r * inv)
        i0, i1, i2 = pieces(jnp.broadcast_to(inv, (depth, rows)))
        scaled = jnp.concatenate([q0, q1, q2, i0, i1, i2], axis=0).astype(BF16)
        p_hi = p.astype(BF16)
        p_lo = (p - p_hi.astype(F32)).astype(BF16)
        high = dot(scaled, p_hi, 1, 1)
        low = dot(scaled, p_lo, 1, 1)
        mass = high[:depth] + (high[depth : 2 * depth] + (high[2 * depth : 3 * depth] + low[:depth]))
        mass = mass + low[depth : 2 * depth]
        o = 3 * depth
        count = high[o : o + 1] + (high[o + depth : o + depth + 1] + low[o : o + 1])
        count = count + high[o + 2 * depth : o + 2 * depth + 1] + low[o + depth : o + depth + 1]
        for d in range(depth):
            owner, slot = divmod(m * depth + d, 3)
            core, xz = divmod(owner, NX * NZL)
            row = xz * NC + core
            out_ref[row, slot : slot + 1, :] = mass[d : d + 1]
            out_ref[row, slot + 3 : slot + 4, :] = count


def update_kernel(place_ref, all_books_ref, parts_ref, out_ref, books_ref, sem):
    x, y, zl, zh, c = (place_ref[i] for i in range(5))
    share = books_ref.shape[0]
    first = pl.multiple_of((y * NZH + zh) * share, 8)
    copy = pltpu.make_async_copy(all_books_ref.at[pl.ds(first, share), :], books_ref, sem)
    copy.start()
    total = jnp.sum(parts_ref[...], axis=0)
    copy.wait()
    row = ((c * NX + x) * NZL + zl) * 3
    old = jnp.concatenate([books_ref[pl.ds(row + i, 1), :] for i in range(3)], axis=0)
    new = (total[:3] + old) / (total[3:6] + 1.0)
    tile = jnp.concatenate([new[:, :128], new[:, 128:], jnp.zeros((2, 128), F32)], axis=0)
    for i in range(out_ref.shape[0]):
        out_ref[i] = tile


def books_kernel(place_ref, mine_ref, theirs_ref, out_ref):
    core = place_ref[4]
    count = mine_ref.shape[0]
    group = NX * NZL

    def place(first_ref, second_ref):
        for side, ref in ((0, first_ref), (1, second_ref)):
            for i in range(count):
                cent, xz = divmod(i, group)
                row = (cent * NC + side) * group * 3 + xz * 3
                out_ref[row : row + 3, :128] = ref[i, :3, :]
                out_ref[row : row + 3, 128:] = ref[i, 3:6, :]

    @pl.when(core == 0)
    def _():
        place(mine_ref, theirs_ref)

    @pl.when(core == 1)
    def _():
        place(theirs_ref, mine_ref)


def centroids_kernel(place_ref, mine_ref, theirs_ref, out_ref):
    spots = relative_blocks(place_ref)
    half = len(spots) // 2
    size = mine_ref.shape[0] // half
    for i, spot in enumerate(spots):
        ref = mine_ref if i < half else theirs_ref
        at = (i % half) * size
        out_ref[pl.ds(pl.multiple_of(spot * size, 8), size), :] = ref[at : at + size, :]


def body(embeddings, centroids, codebooks):
    rows_here, width = embeddings.shape
    held = centroids.shape[0]
    subspaces, depth, codes = codebooks.shape
    row_at = lax.axis_index("rows")
    cent_at = lax.axis_index("cent")
    x, zl, c = row_at // (NZL * NC), (row_at // NC) % NZL, row_at % NC
    y, zh = cent_at // NZH, cent_at % NZH
    place = jnp.stack([x, y, zl, zh, c]).astype(jnp.int32)
    cents = NY * NZH
    share = width // cents

    p, stat, cent_t, old = call(
        logits_kernel,
        (
            shape((held, rows_here)),
            shape((cents, 2 * rows_here // 128, 128)),
            shape((width, held), BF16),
            shape((held // (NC * NX * NZL), width)),
        ),
        (place, embeddings, centroids),
        smem=1,
        scratch=(pltpu.VMEM((held, width), BF16),),
        flops=2 * rows_here * held * width,
    )
    stats = lax.all_to_all(stat, "cent", 0, 0, tiled=True)
    outs = call(
        weights_kernel,
        (shape((held, rows_here), BF16), shape((held, 128))) + (shape((share, rows_here)),) * 8,
        (place, p, stat, stats, cent_t),
        smem=1,
        flops=2 * rows_here * held * width,
    )
    wb, counts, theirs, mine = outs[0], outs[1], outs[2:6], outs[6:10]
    steps = (1, -1, 2)
    got = [hop(theirs[k % NY], along_y(k)) for k in steps]
    got_mine = [hop(mine[k % NY], along_y(k)) for k in steps]
    peer = hop(call(add_kernel, shape((share, rows_here)), (theirs[0], *got)), other_zh)

    keep, send, emb_t = call(
        mass_kernel,
        (shape((held // 2, width + 128)),) * 2 + (shape((share, rows_here)),),
        (place, wb, counts, embeddings),
        smem=1,
        scratch=(pltpu.VMEM((width, rows_here), BF16),),
        flops=2 * rows_here * held * width,
    )
    for step, move in enumerate((other_core, along_x(2), along_x(1), along_zl(2))):
        half = keep.shape[0] // 2
        got = hop(send, move)
        keep, send = call(halve_kernel, (shape((half, width + 128)),) * 2, (keep, got), limit=4)
        if step == 2:
            send, peer = lax.optimization_barrier((send, peer))
    peers = NX * NZL

    per = subspaces // cents
    sums = call(
        codebook_kernel,
        shape((NX * NZL * NC, 8, codes)),
        (place, codebooks, emb_t, mine[0], *got_mine, peer),
        smem=1,
        hbm_in=1,
        scratch=(pltpu.VMEM((per, depth, codes), F32), pltpu.SemaphoreType.DMA),
        flops=64 * rows_here * per * codes * 64,
    )
    sums, keep = lax.optimization_barrier((sums, keep))
    new = call(
        centroid_kernel, shape((half, width)), (keep, hop(send, along_zl(1)), old), limit=4
    )
    new_z = jnp.concatenate([new] + [hop(new, along_zl(k)) for k in (1, 2, 3)], axis=0)
    all_parts = lax.all_to_all(sums, "rows", 0, 0, tiled=True)
    same_core = [
        [flat(xx, yy, zz, hh, cc) for yy in range(NY) for hh in range(NZH) for xx in range(NX) for zz in range(NZL)]
        for cc in range(NC)
    ]
    tile = call(
        update_kernel,
        shape((cents * peers, 8, 128)),
        (place, codebooks.reshape(subspaces * depth, codes), all_parts),
        smem=1,
        hbm_in=1,
        scratch=(pltpu.VMEM((share, codes), F32), pltpu.SemaphoreType.DMA),
    )
    new_x = jnp.concatenate([new_z] + [hop(new_z, along_x(k)) for k in (1, 2, 3)], axis=0)
    tile, new_z = lax.optimization_barrier((tile, new_z))
    new_other = hop(new_x, other_core)
    new_centroids = call(
        centroids_kernel, shape((held, width)), (place, new_x, new_other), smem=1
    )
    tiles = lax.all_to_all(tile, BOTH, 0, 0, tiled=True, axis_index_groups=same_core)
    tiles_other = hop(tiles, other_core)
    new_books = call(
        books_kernel, shape((subspaces * depth, codes)), (place, tiles, tiles_other), smem=1
    )
    return (new_centroids, new_books.reshape(codebooks.shape))


def solution(mesh):
    in_specs = (P("rows", None), P("cent", None), P())
    out_specs = (P("cent", None), P())
    return jax.shard_map(body, mesh=mesh, in_specs=in_specs, out_specs=out_specs, check_vma=False)
```

```python
import functools
import itertools
import math

import jax
import jax.numpy as jnp
from jax import lax
from jax.experimental import pallas as pl
from jax.experimental.pallas import tpu as pltpu
from jax.sharding import PartitionSpec as P

NX, NY, NZL, NZH, NC = 4, 4, 4, 2, 2
BOTH = ("rows", "cent")
F32, BF16 = jnp.float32, jnp.bfloat16


def flat(x, y, zl, zh, c):
    return ((x * NZL + zl) * NC + c) * (NY * NZH) + (y * NZH + zh)


def hop(value, move):
    pairs = []
    for place in itertools.product(range(NX), range(NY), range(NZL), range(NZH), range(NC)):
        pairs.append((flat(*place), flat(*move(*place))))
    return lax.ppermute(value, BOTH, pairs)


def along_x(k):
    return lambda x, y, zl, zh, c: (x ^ k, y, zl, zh, c)


def along_y(k):
    return lambda x, y, zl, zh, c: (x, (y + k) % NY, zl, zh, c)


def along_zl(k):
    return lambda x, y, zl, zh, c: (x, y, zl ^ k, zh, c)


def other_zh(x, y, zl, zh, c):
    return (x, y, zl, 1 - zh, c)


def other_core(x, y, zl, zh, c):
    return (x, y, zl, zh, 1 - c)


def call(kernel, out, args, smem=0, scratch=(), flops=0, limit=12, hbm_in=0):
    nbytes = sum(a.size * a.dtype.itemsize for a in args)
    specs = [pl.BlockSpec(memory_space=pltpu.SMEM)] * smem
    specs += [pl.BlockSpec(memory_space=pl.ANY)] * hbm_in
    specs += [pl.BlockSpec(memory_space=pltpu.VMEM)] * (len(args) - smem - hbm_in)
    return pl.pallas_call(
        kernel,
        out_shape=out,
        in_specs=specs,
        out_specs=jax.tree.map(lambda _: pl.BlockSpec(memory_space=pltpu.VMEM), out),
        scratch_shapes=list(scratch),
        compiler_params=pltpu.CompilerParams(vmem_limit_bytes=limit * 1024 * 1024),
        cost_estimate=pl.CostEstimate(flops=flops, bytes_accessed=2 * nbytes, transcendentals=0),
    )(*args)


def shape(dims, dtype=F32):
    return jax.ShapeDtypeStruct(dims, dtype)


def dot(a, b, ca, cb):
    return lax.dot_general(a, b, (((ca,), (cb,)), ((), ())), preferred_element_type=F32)


def relative_blocks(place_ref):
    x, zl, c = place_ref[0], place_ref[2], place_ref[4]
    spots = []
    for kc, kx, kz in itertools.product(range(NC), range(NX), range(NZL)):
        spot = (lax.bitwise_xor(c, kc) * NX + lax.bitwise_xor(x, kx)) * NZL + lax.bitwise_xor(zl, kz)
        spots.append(spot)
    return spots


def logits_kernel(place_ref, emb_ref, cent_ref, p_ref, stat_ref, cent_t_ref, old_ref, held_ref):
    rows, width = emb_ref.shape
    step = 256
    spots = relative_blocks(place_ref)
    size = cent_ref.shape[0] // len(spots)
    for i, spot in enumerate(spots):
        held_ref[i * size : (i + 1) * size, :] = cent_ref[pl.ds(pl.multiple_of(spot * size, 16), size), :]
    cent = held_ref[...]
    cent_t_ref[...] = cent.T
    old_ref[...] = cent[:size, :].astype(F32)
    cent_f = cent.astype(F32)
    half_sq = 0.5 * jnp.sum(cent_f * cent_f, axis=1, keepdims=True)
    tops, sums = [], []
    for start in range(0, rows, step):
        cross = dot(cent, emb_ref[start : start + step, :], 1, 1)
        logits = (cross - half_sq) * (3.0 / math.sqrt(width))
        top = jnp.max(logits, axis=0, keepdims=True)
        p = jnp.exp(logits - top)
        p_ref[:, start : start + step] = p
        tops.append(top)
        sums.append(jnp.sum(p, axis=0, keepdims=True))
    block = jnp.concatenate(
        [
            jnp.concatenate(tops, axis=1).reshape(rows // 128, 128),
            jnp.concatenate(sums, axis=1).reshape(rows // 128, 128),
        ],
        axis=0,
    )
    for i in range(stat_ref.shape[0]):
        stat_ref[i] = block


def weights_kernel(place_ref, p_ref, mine_ref, stat_ref, cent_t_ref, wb_ref, count_ref, *out_refs):
    y, zh = place_ref[1], place_ref[3]
    half = stat_ref.shape[1] // 2
    tops = stat_ref[:, :half, :]
    top = jnp.max(tops, axis=0)
    total = jnp.sum(stat_ref[:, half:, :] * jnp.exp(tops - top[None]), axis=0)
    scale = jnp.exp(mine_ref[0, :half, :] - top) / total
    scale = scale.reshape(1, p_ref.shape[1])
    w = p_ref[...] * scale
    count_ref[...] = jnp.broadcast_to(jnp.sum(w, axis=1, keepdims=True), count_ref.shape)
    wb_ref[...] = w.astype(BF16)
    share = out_refs[0].shape[0]
    for part in range(2):
        for k in range(NY):
            side = (1 - zh) if part == 0 else zh
            start = ((y + k) % NY) * (NZH * share) + side * share
            piece = cent_t_ref[pl.ds(pl.multiple_of(start, 16), share), :]
            out_refs[part * NY + k][...] = dot(piece, wb_ref[...], 1, 0)


def mass_kernel(place_ref, wb_ref, count_ref, emb_ref, keep_ref, send_ref, emb_t_ref, turned_ref):
    half, width = keep_ref.shape[0], emb_ref.shape[1]
    for ref, start in ((send_ref, half), (keep_ref, 0)):
        ref[:, :width] = dot(wb_ref[start : start + half, :], emb_ref[...], 1, 0)
        ref[:, width:] = count_ref[start : start + half, :]
    share = emb_t_ref.shape[0]
    turned_ref[...] = emb_ref[...].T
    first = (place_ref[1] * NZH + place_ref[3]) * share
    emb_t_ref[...] = turned_ref[pl.ds(pl.multiple_of(first, 16), share), :].astype(F32)


def halve_kernel(mine_ref, got_ref, keep_ref, send_ref):
    half = keep_ref.shape[0]
    keep_ref[...] = mine_ref[:half, :] + got_ref[:half, :]
    send_ref[...] = mine_ref[half:, :] + got_ref[half:, :]


def centroid_kernel(mine_ref, got_ref, old_ref, out_ref):
    rows, width = out_ref.shape
    total = mine_ref[...] + got_ref[...]
    out_ref[...] = (total[:, :width] + old_ref[...]) / (total[:, width : width + 1] + 1.0)


def add_kernel(a_ref, b_ref, c_ref, d_ref, out_ref):
    out_ref[...] = (a_ref[...] + b_ref[...]) + (c_ref[...] + d_ref[...])


def pieces(v):
    hi = v.astype(BF16).astype(F32)
    rest = v - hi
    mid = rest.astype(BF16).astype(F32)
    return hi, mid, rest - mid


def codebook_kernel(
    side, place_ref, all_books_ref, emb_t_ref, a_ref, b_ref, c_ref, d_ref, e_ref, *refs
):
    out_ref, books_ref, sem = refs[-3:]
    subspaces, depth, codes = books_ref.shape
    first = (place_ref[1] * NZH + place_ref[3]) * subspaces
    if side:
        for xz in range(NX * NZL):
            out_ref[xz * NC] = refs[0][xz * NC]
    copy = pltpu.make_async_copy(all_books_ref.at[pl.ds(first, subspaces)], books_ref, sem)
    copy.start()
    copy.wait()
    rows = emb_t_ref.shape[1]
    ones = jnp.where(lax.broadcasted_iota(jnp.int32, (2 * depth, rows), 0) < 3, 1.0, 0.0)
    half = subspaces // 2
    for m in range(side * half, (side + 1) * half):
        at = slice(m * depth, (m + 1) * depth)
        recon = a_ref[at, :] + b_ref[at, :] + c_ref[at, :] + d_ref[at, :] + e_ref[at, :]
        r = emb_t_ref[at, :] - recon
        r0, r1, r2 = pieces(r)
        book = books_ref[m]
        k0, k1, k2 = pieces(book)
        s0, s1, s2 = pieces(-0.5 * jnp.sum(book * book, axis=0, keepdims=True))
        zero = jnp.zeros((2 * depth - 3, codes), F32)
        left = jnp.concatenate([k0, k0, k1, k0, k2, k1, s0, s1, s2, zero], axis=0).astype(BF16)
        right = jnp.concatenate([r0, r1, r0, r2, r0, r1, ones], axis=0).astype(BF16)
        logits = dot(left, right, 0, 0)
        p = jnp.exp(logits - jnp.max(logits, axis=0, keepdims=True))
        inv = 1.0 / jnp.sum(p, axis=0, keepdims=True)
        q0, q1, q2 = pieces(r * inv)
        i0, i1, i2 = pieces(jnp.broadcast_to(inv, (depth, rows)))
        scaled = jnp.concatenate([q0, q1, q2, i0, i1, i2], axis=0).astype(BF16)
        p_hi = p.astype(BF16)
        p_lo = (p - p_hi.astype(F32)).astype(BF16)
        high = dot(scaled, p_hi, 1, 1)
        low = dot(scaled, p_lo, 1, 1)
        mass = high[:depth] + (high[depth : 2 * depth] + (high[2 * depth : 3 * depth] + low[:depth]))
        mass = mass + low[depth : 2 * depth]
        o = 3 * depth
        count = high[o : o + 1] + (high[o + depth : o + depth + 1] + low[o : o + 1])
        count = count + high[o + 2 * depth : o + 2 * depth + 1] + low[o + depth : o + depth + 1]
        for d in range(depth):
            owner, slot = divmod(m * depth + d, 3)
            core, xz = divmod(owner, NX * NZL)
            row = xz * NC + core
            out_ref[row, slot : slot + 1, :] = mass[d : d + 1]
            out_ref[row, slot + 3 : slot + 4, :] = count


def update_kernel(place_ref, all_books_ref, parts_ref, out_ref, books_ref, sem):
    x, y, zl, zh, c = (place_ref[i] for i in range(5))
    share = books_ref.shape[0]
    first = pl.multiple_of((y * NZH + zh) * share, 8)
    copy = pltpu.make_async_copy(all_books_ref.at[pl.ds(first, share), :], books_ref, sem)
    copy.start()
    total = jnp.sum(parts_ref[...], axis=0)
    copy.wait()
    row = ((c * NX + x) * NZL + zl) * 3
    old = jnp.concatenate([books_ref[pl.ds(row + i, 1), :] for i in range(3)], axis=0)
    new = (total[:3] + old) / (total[3:6] + 1.0)
    tile = jnp.concatenate([new[:, :128], new[:, 128:], jnp.zeros((2, 128), F32)], axis=0)
    for i in range(out_ref.shape[0]):
        out_ref[i] = tile


def books_kernel(place_ref, mine_ref, theirs_ref, out_ref):
    core = place_ref[4]
    count = mine_ref.shape[0]
    group = NX * NZL

    def place(first_ref, second_ref):
        for side, ref in ((0, first_ref), (1, second_ref)):
            for i in range(count):
                cent, xz = divmod(i, group)
                row = (cent * NC + side) * group * 3 + xz * 3
                out_ref[row : row + 3, :128] = ref[i, :3, :]
                out_ref[row : row + 3, 128:] = ref[i, 3:6, :]

    @pl.when(core == 0)
    def _():
        place(mine_ref, theirs_ref)

    @pl.when(core == 1)
    def _():
        place(theirs_ref, mine_ref)


def centroids_kernel(place_ref, mine_ref, theirs_ref, out_ref):
    spots = relative_blocks(place_ref)
    half = len(spots) // 2
    size = mine_ref.shape[0] // half
    for i, spot in enumerate(spots):
        ref = mine_ref if i < half else theirs_ref
        at = (i % half) * size
        out_ref[pl.ds(pl.multiple_of(spot * size, 8), size), :] = ref[at : at + size, :]


def body(embeddings, centroids, codebooks):
    rows_here, width = embeddings.shape
    held = centroids.shape[0]
    subspaces, depth, codes = codebooks.shape
    row_at = lax.axis_index("rows")
    cent_at = lax.axis_index("cent")
    x, zl, c = row_at // (NZL * NC), (row_at // NC) % NZL, row_at % NC
    y, zh = cent_at // NZH, cent_at % NZH
    place = jnp.stack([x, y, zl, zh, c]).astype(jnp.int32)
    cents = NY * NZH
    share = width // cents

    p, stat, cent_t, old = call(
        logits_kernel,
        (
            shape((held, rows_here)),
            shape((cents, 2 * rows_here // 128, 128)),
            shape((width, held), BF16),
            shape((held // (NC * NX * NZL), width)),
        ),
        (place, embeddings, centroids),
        smem=1,
        scratch=(pltpu.VMEM((held, width), BF16),),
        flops=2 * rows_here * held * width,
    )
    stats = lax.all_to_all(stat, "cent", 0, 0, tiled=True)
    outs = call(
        weights_kernel,
        (shape((held, rows_here), BF16), shape((held, 128))) + (shape((share, rows_here)),) * 8,
        (place, p, stat, stats, cent_t),
        smem=1,
        flops=2 * rows_here * held * width,
    )
    wb, counts, theirs, mine = outs[0], outs[1], outs[2:6], outs[6:10]
    steps = (1, -1, 2)
    got = [hop(theirs[k % NY], along_y(k)) for k in steps]
    got_mine = [hop(mine[k % NY], along_y(k)) for k in steps]
    peer = hop(call(add_kernel, shape((share, rows_here)), (theirs[0], *got)), other_zh)

    keep, send, emb_t = call(
        mass_kernel,
        (shape((held // 2, width + 128)),) * 2 + (shape((share, rows_here)),),
        (place, wb, counts, embeddings),
        smem=1,
        scratch=(pltpu.VMEM((width, rows_here), BF16),),
        flops=2 * rows_here * held * width,
    )
    for move in (other_core, along_x(2), along_x(1)):
        half = keep.shape[0] // 2
        got = hop(send, move)
        keep, send = call(halve_kernel, (shape((half, width + 128)),) * 2, (keep, got), limit=4)
    peers = NX * NZL
    per = subspaces // cents

    def codebook_half(side, *more):
        return call(
            functools.partial(codebook_kernel, side),
            shape((NX * NZL * NC, 8, codes)),
            (place, codebooks, emb_t, mine[0], *got_mine, peer, *more),
            smem=1,
            hbm_in=1,
            scratch=(pltpu.VMEM((per, depth, codes), F32), pltpu.SemaphoreType.DMA),
            flops=64 * rows_here * per * codes * 64,
        )

    send, peer = lax.optimization_barrier((send, peer))
    got = hop(send, along_zl(2))
    first_sums = codebook_half(0)
    first_sums, got = lax.optimization_barrier((first_sums, got))
    half = keep.shape[0] // 2
    keep, send = call(halve_kernel, (shape((half, width + 128)),) * 2, (keep, got), limit=4)
    got = hop(send, along_zl(1))
    sums = codebook_half(1, first_sums)
    sums, got = lax.optimization_barrier((sums, got))
    new = call(
        centroid_kernel, shape((half, width)), (keep, got, old), limit=4
    )
    new_z = jnp.concatenate([new] + [hop(new, along_zl(k)) for k in (1, 2, 3)], axis=0)
    all_parts = lax.all_to_all(sums, "rows", 0, 0, tiled=True)
    same_core = [
        [flat(xx, yy, zz, hh, cc) for yy in range(NY) for hh in range(NZH) for xx in range(NX) for zz in range(NZL)]
        for cc in range(NC)
    ]
    tile = call(
        update_kernel,
        shape((cents * peers, 8, 128)),
        (place, codebooks.reshape(subspaces * depth, codes), all_parts),
        smem=1,
        hbm_in=1,
        scratch=(pltpu.VMEM((share, codes), F32), pltpu.SemaphoreType.DMA),
    )
    new_x = jnp.concatenate([new_z] + [hop(new_z, along_x(k)) for k in (1, 2, 3)], axis=0)
    new_other = hop(new_x, other_core)
    new_centroids = call(
        centroids_kernel, shape((held, width)), (place, new_x, new_other), smem=1
    )
    tiles = lax.all_to_all(tile, BOTH, 0, 0, tiled=True, axis_index_groups=same_core)
    tiles_other = hop(tiles, other_core)
    new_books = call(
        books_kernel, shape((subspaces * depth, codes)), (place, tiles, tiles_other), smem=1
    )
    return (new_centroids, new_books.reshape(codebooks.shape))


def solution(mesh):
    in_specs = (P("rows", None), P("cent", None), P())
    out_specs = (P("cent", None), P())
    return jax.shard_map(body, mesh=mesh, in_specs=in_specs, out_specs=out_specs, check_vma=False)
```

```python
import itertools
import math

import jax
import jax.numpy as jnp
from jax import lax
from jax.experimental import pallas as pl
from jax.experimental.pallas import tpu as pltpu
from jax.sharding import PartitionSpec as P

NX, NY, NZL, NZH, NC = 4, 4, 4, 2, 2
BOTH = ("rows", "cent")
F32, BF16 = jnp.float32, jnp.bfloat16


def flat(x, y, zl, zh, c):
    return ((x * NZL + zl) * NC + c) * (NY * NZH) + (y * NZH + zh)


def hop(value, move):
    pairs = []
    for place in itertools.product(range(NX), range(NY), range(NZL), range(NZH), range(NC)):
        pairs.append((flat(*place), flat(*move(*place))))
    return lax.ppermute(value, BOTH, pairs)


def along_x(k):
    return lambda x, y, zl, zh, c: (x ^ k, y, zl, zh, c)


def along_y(k):
    return lambda x, y, zl, zh, c: (x, (y + k) % NY, zl, zh, c)


def along_zl(k):
    return lambda x, y, zl, zh, c: (x, y, zl ^ k, zh, c)


def other_zh(x, y, zl, zh, c):
    return (x, y, zl, 1 - zh, c)


def other_core(x, y, zl, zh, c):
    return (x, y, zl, zh, 1 - c)


def call(kernel, out, args, smem=0, scratch=(), flops=0, limit=12, hbm_in=0):
    nbytes = sum(a.size * a.dtype.itemsize for a in args)
    specs = [pl.BlockSpec(memory_space=pltpu.SMEM)] * smem
    specs += [pl.BlockSpec(memory_space=pl.ANY)] * hbm_in
    specs += [pl.BlockSpec(memory_space=pltpu.VMEM)] * (len(args) - smem - hbm_in)
    return pl.pallas_call(
        kernel,
        out_shape=out,
        in_specs=specs,
        out_specs=jax.tree.map(lambda _: pl.BlockSpec(memory_space=pltpu.VMEM), out),
        scratch_shapes=list(scratch),
        compiler_params=pltpu.CompilerParams(vmem_limit_bytes=limit * 1024 * 1024),
        cost_estimate=pl.CostEstimate(flops=flops, bytes_accessed=2 * nbytes, transcendentals=0),
    )(*args)


def shape(dims, dtype=F32):
    return jax.ShapeDtypeStruct(dims, dtype)


def dot(a, b, ca, cb):
    return lax.dot_general(a, b, (((ca,), (cb,)), ((), ())), preferred_element_type=F32)


def relative_blocks(place_ref):
    x, zl, c = place_ref[0], place_ref[2], place_ref[4]
    spots = []
    for kc, kx, kz in itertools.product(range(NC), range(NX), range(NZL)):
        spot = (lax.bitwise_xor(c, kc) * NX + lax.bitwise_xor(x, kx)) * NZL + lax.bitwise_xor(zl, kz)
        spots.append(spot)
    return spots


def logits_kernel(place_ref, emb_ref, cent_ref, p_ref, stat_ref, cent_t_ref, old_ref, held_ref):
    rows, width = emb_ref.shape
    step = 256
    spots = relative_blocks(place_ref)
    size = cent_ref.shape[0] // len(spots)
    for i, spot in enumerate(spots):
        held_ref[i * size : (i + 1) * size, :] = cent_ref[pl.ds(pl.multiple_of(spot * size, 16), size), :]
    cent = held_ref[...]
    cent_t_ref[...] = cent.T
    old_ref[...] = cent[:size, :].astype(F32)
    cent_f = cent.astype(F32)
    half_sq = 0.5 * jnp.sum(cent_f * cent_f, axis=1, keepdims=True)
    tops, sums = [], []
    for start in range(0, rows, step):
        cross = dot(cent, emb_ref[start : start + step, :], 1, 1)
        logits = (cross - half_sq) * (3.0 / math.sqrt(width))
        top = jnp.max(logits, axis=0, keepdims=True)
        p = jnp.exp(logits - top)
        p_ref[:, start : start + step] = p
        tops.append(top)
        sums.append(jnp.sum(p, axis=0, keepdims=True))
    block = jnp.concatenate(
        [
            jnp.concatenate(tops, axis=1).reshape(rows // 128, 128),
            jnp.concatenate(sums, axis=1).reshape(rows // 128, 128),
        ],
        axis=0,
    )
    for i in range(stat_ref.shape[0]):
        stat_ref[i] = block


def weights_kernel(place_ref, p_ref, mine_ref, stat_ref, cent_t_ref, wb_ref, count_ref, *out_refs):
    y, zh = place_ref[1], place_ref[3]
    half = stat_ref.shape[1] // 2
    tops = stat_ref[:, :half, :]
    top = jnp.max(tops, axis=0)
    total = jnp.sum(stat_ref[:, half:, :] * jnp.exp(tops - top[None]), axis=0)
    scale = jnp.exp(mine_ref[0, :half, :] - top) / total
    scale = scale.reshape(1, p_ref.shape[1])
    w = p_ref[...] * scale
    count_ref[...] = jnp.broadcast_to(jnp.sum(w, axis=1, keepdims=True), count_ref.shape)
    wb_ref[...] = w.astype(BF16)
    share = out_refs[0].shape[0]
    for part in range(2):
        for k in range(NY):
            side = (1 - zh) if part == 0 else zh
            start = ((y + k) % NY) * (NZH * share) + side * share
            piece = cent_t_ref[pl.ds(pl.multiple_of(start, 16), share), :]
            out_refs[part * NY + k][...] = dot(piece, wb_ref[...], 1, 0)


def mass_kernel(place_ref, wb_ref, count_ref, emb_ref, keep_ref, send_ref, emb_t_ref, turned_ref):
    half, width = keep_ref.shape[0], emb_ref.shape[1]
    for ref, start in ((send_ref, half), (keep_ref, 0)):
        ref[:, :width] = dot(wb_ref[start : start + half, :], emb_ref[...], 1, 0)
        ref[:, width:] = count_ref[start : start + half, :]
    share = emb_t_ref.shape[0]
    turned_ref[...] = emb_ref[...].T
    first = (place_ref[1] * NZH + place_ref[3]) * share
    emb_t_ref[...] = turned_ref[pl.ds(pl.multiple_of(first, 16), share), :].astype(F32)


def halve_kernel(mine_ref, got_ref, keep_ref, send_ref):
    half = keep_ref.shape[0]
    keep_ref[...] = mine_ref[:half, :] + got_ref[:half, :]
    send_ref[...] = mine_ref[half:, :] + got_ref[half:, :]


def centroid_kernel(mine_ref, got_ref, old_ref, out_ref):
    rows, width = out_ref.shape
    total = mine_ref[...] + got_ref[...]
    out_ref[...] = (total[:, :width] + old_ref[...]) / (total[:, width : width + 1] + 1.0)


def add_kernel(a_ref, b_ref, c_ref, d_ref, out_ref):
    out_ref[...] = (a_ref[...] + b_ref[...]) + (c_ref[...] + d_ref[...])


def pieces(v):
    hi = v.astype(BF16).astype(F32)
    rest = v - hi
    mid = rest.astype(BF16).astype(F32)
    return hi, mid, rest - mid


def codebook_kernel(
    place_ref, all_books_ref, emb_t_ref, a_ref, b_ref, c_ref, d_ref, e_ref, out_ref, books_ref, sem
):
    subspaces, depth, codes = books_ref.shape
    first = (place_ref[1] * NZH + place_ref[3]) * subspaces
    copy = pltpu.make_async_copy(all_books_ref.at[pl.ds(first, subspaces)], books_ref, sem)
    copy.start()
    copy.wait()
    rows = emb_t_ref.shape[1]
    ones = jnp.where(lax.broadcasted_iota(jnp.int32, (2 * depth, rows), 0) < 3, 1.0, 0.0)
    for m in range(subspaces):
        at = slice(m * depth, (m + 1) * depth)
        recon = a_ref[at, :] + b_ref[at, :] + c_ref[at, :] + d_ref[at, :] + e_ref[at, :]
        r = emb_t_ref[at, :] - recon
        r0, r1, r2 = pieces(r)
        book = books_ref[m]
        k0, k1, k2 = pieces(book)
        s0, s1, s2 = pieces(-0.5 * jnp.sum(book * book, axis=0, keepdims=True))
        zero = jnp.zeros((2 * depth - 3, codes), F32)
        left = jnp.concatenate([k0, k0, k1, k0, k2, k1, s0, s1, s2, zero], axis=0).astype(BF16)
        right = jnp.concatenate([r0, r1, r0, r2, r0, r1, ones], axis=0).astype(BF16)
        logits = dot(left, right, 0, 0)
        p = jnp.exp(logits - jnp.max(logits, axis=0, keepdims=True))
        inv = 1.0 / jnp.sum(p, axis=0, keepdims=True)
        q0, q1, q2 = pieces(r * inv)
        i0, i1, i2 = pieces(jnp.broadcast_to(inv, (depth, rows)))
        scaled = jnp.concatenate([q0, q1, q2, i0, i1, i2], axis=0).astype(BF16)
        p_hi = p.astype(BF16)
        high = dot(scaled, p_hi, 1, 1)
        mass = high[:depth] + (high[depth : 2 * depth] + high[2 * depth : 3 * depth])
        o = 3 * depth
        count = high[o : o + 1] + (high[o + depth : o + depth + 1] + high[o + 2 * depth : o + 2 * depth + 1])
        for d in range(depth):
            owner, slot = divmod(m * depth + d, 3)
            core, xz = divmod(owner, NX * NZL)
            row = xz * NC + core
            out_ref[row, slot : slot + 1, :] = mass[d : d + 1]
            out_ref[row, slot + 3 : slot + 4, :] = count


def update_kernel(place_ref, all_books_ref, parts_ref, out_ref, books_ref, sem):
    x, y, zl, zh, c = (place_ref[i] for i in range(5))
    share = books_ref.shape[0]
    first = pl.multiple_of((y * NZH + zh) * share, 8)
    copy = pltpu.make_async_copy(all_books_ref.at[pl.ds(first, share), :], books_ref, sem)
    copy.start()
    total = jnp.sum(parts_ref[...], axis=0)
    copy.wait()
    row = ((c * NX + x) * NZL + zl) * 3
    old = jnp.concatenate([books_ref[pl.ds(row + i, 1), :] for i in range(3)], axis=0)
    new = (total[:3] + old) / (total[3:6] + 1.0)
    tile = jnp.concatenate([new[:, :128], new[:, 128:], jnp.zeros((2, 128), F32)], axis=0)
    for i in range(out_ref.shape[0]):
        out_ref[i] = tile


def books_kernel(place_ref, mine_ref, theirs_ref, out_ref):
    core = place_ref[4]
    count = mine_ref.shape[0]
    group = NX * NZL

    def place(first_ref, second_ref):
        for side, ref in ((0, first_ref), (1, second_ref)):
            for i in range(count):
                cent, xz = divmod(i, group)
                row = (cent * NC + side) * group * 3 + xz * 3
                out_ref[row : row + 3, :128] = ref[i, :3, :]
                out_ref[row : row + 3, 128:] = ref[i, 3:6, :]

    @pl.when(core == 0)
    def _():
        place(mine_ref, theirs_ref)

    @pl.when(core == 1)
    def _():
        place(theirs_ref, mine_ref)


def centroids_kernel(place_ref, mine_ref, theirs_ref, out_ref):
    spots = relative_blocks(place_ref)
    half = len(spots) // 2
    size = mine_ref.shape[0] // half
    for i, spot in enumerate(spots):
        ref = mine_ref if i < half else theirs_ref
        at = (i % half) * size
        out_ref[pl.ds(pl.multiple_of(spot * size, 8), size), :] = ref[at : at + size, :]


def body(embeddings, centroids, codebooks):
    rows_here, width = embeddings.shape
    held = centroids.shape[0]
    subspaces, depth, codes = codebooks.shape
    row_at = lax.axis_index("rows")
    cent_at = lax.axis_index("cent")
    x, zl, c = row_at // (NZL * NC), (row_at // NC) % NZL, row_at % NC
    y, zh = cent_at // NZH, cent_at % NZH
    place = jnp.stack([x, y, zl, zh, c]).astype(jnp.int32)
    cents = NY * NZH
    share = width // cents

    p, stat, cent_t, old = call(
        logits_kernel,
        (
            shape((held, rows_here)),
            shape((cents, 2 * rows_here // 128, 128)),
            shape((width, held), BF16),
            shape((held // (NC * NX * NZL), width)),
        ),
        (place, embeddings, centroids),
        smem=1,
        scratch=(pltpu.VMEM((held, width), BF16),),
        flops=2 * rows_here * held * width,
    )
    stats = lax.all_to_all(stat, "cent", 0, 0, tiled=True)
    outs = call(
        weights_kernel,
        (shape((held, rows_here), BF16), shape((held, 128))) + (shape((share, rows_here)),) * 8,
        (place, p, stat, stats, cent_t),
        smem=1,
        flops=2 * rows_here * held * width,
    )
    wb, counts, theirs, mine = outs[0], outs[1], outs[2:6], outs[6:10]
    steps = (1, -1, 2)
    got = [hop(theirs[k % NY], along_y(k)) for k in steps]
    got_mine = [hop(mine[k % NY], along_y(k)) for k in steps]
    peer = hop(call(add_kernel, shape((share, rows_here)), (theirs[0], *got)), other_zh)

    keep, send, emb_t = call(
        mass_kernel,
        (shape((held // 2, width + 128)),) * 2 + (shape((share, rows_here)),),
        (place, wb, counts, embeddings),
        smem=1,
        scratch=(pltpu.VMEM((width, rows_here), BF16),),
        flops=2 * rows_here * held * width,
    )
    for step, move in enumerate((other_core, along_x(2), along_x(1), along_zl(2))):
        half = keep.shape[0] // 2
        got = hop(send, move)
        keep, send = call(halve_kernel, (shape((half, width + 128)),) * 2, (keep, got), limit=4)
        if step == 2:
            send, peer = lax.optimization_barrier((send, peer))
    peers = NX * NZL

    per = subspaces // cents
    sums = call(
        codebook_kernel,
        shape((NX * NZL * NC, 8, codes)),
        (place, codebooks, emb_t, mine[0], *got_mine, peer),
        smem=1,
        hbm_in=1,
        scratch=(pltpu.VMEM((per, depth, codes), F32), pltpu.SemaphoreType.DMA),
        flops=64 * rows_here * per * codes * 64,
    )
    sums, keep = lax.optimization_barrier((sums, keep))
    new = call(
        centroid_kernel, shape((half, width)), (keep, hop(send, along_zl(1)), old), limit=4
    )
    new_z = jnp.concatenate([new] + [hop(new, along_zl(k)) for k in (1, 2, 3)], axis=0)
    all_parts = lax.all_to_all(sums, "rows", 0, 0, tiled=True)
    same_core = [
        [flat(xx, yy, zz, hh, cc) for yy in range(NY) for hh in range(NZH) for xx in range(NX) for zz in range(NZL)]
        for cc in range(NC)
    ]
    tile = call(
        update_kernel,
        shape((cents * peers, 8, 128)),
        (place, codebooks.reshape(subspaces * depth, codes), all_parts),
        smem=1,
        hbm_in=1,
        scratch=(pltpu.VMEM((share, codes), F32), pltpu.SemaphoreType.DMA),
    )
    new_x = jnp.concatenate([new_z] + [hop(new_z, along_x(k)) for k in (1, 2, 3)], axis=0)
    new_other = hop(new_x, other_core)
    new_centroids = call(
        centroids_kernel, shape((held, width)), (place, new_x, new_other), smem=1
    )
    tiles = lax.all_to_all(tile, BOTH, 0, 0, tiled=True, axis_index_groups=same_core)
    tiles_other = hop(tiles, other_core)
    new_books = call(
        books_kernel, shape((subspaces * depth, codes)), (place, tiles, tiles_other), smem=1
    )
    return (new_centroids, new_books.reshape(codebooks.shape))


def solution(mesh):
    in_specs = (P("rows", None), P("cent", None), P())
    out_specs = (P("cent", None), P())
    return jax.shard_map(body, mesh=mesh, in_specs=in_specs, out_specs=out_specs, check_vma=False)
```

```python
import itertools
import math

import jax
import jax.numpy as jnp
from jax import lax
from jax.experimental import pallas as pl
from jax.experimental.pallas import tpu as pltpu
from jax.sharding import PartitionSpec as P

NX, NY, NZL, NZH, NC = 4, 4, 4, 2, 2
BOTH = ("rows", "cent")
F32, BF16 = jnp.float32, jnp.bfloat16


def flat(x, y, zl, zh, c):
    return ((x * NZL + zl) * NC + c) * (NY * NZH) + (y * NZH + zh)


def hop(value, move):
    pairs = []
    for place in itertools.product(range(NX), range(NY), range(NZL), range(NZH), range(NC)):
        pairs.append((flat(*place), flat(*move(*place))))
    return lax.ppermute(value, BOTH, pairs)


def along_x(k):
    return lambda x, y, zl, zh, c: (x ^ k, y, zl, zh, c)


def along_y(k):
    return lambda x, y, zl, zh, c: (x, (y + k) % NY, zl, zh, c)


def along_zl(k):
    return lambda x, y, zl, zh, c: (x, y, zl ^ k, zh, c)


def other_zh(x, y, zl, zh, c):
    return (x, y, zl, 1 - zh, c)


def other_core(x, y, zl, zh, c):
    return (x, y, zl, zh, 1 - c)


def call(kernel, out, args, smem=0, scratch=(), flops=0, limit=12, hbm_in=0):
    nbytes = sum(a.size * a.dtype.itemsize for a in args)
    specs = [pl.BlockSpec(memory_space=pltpu.SMEM)] * smem
    specs += [pl.BlockSpec(memory_space=pl.ANY)] * hbm_in
    specs += [pl.BlockSpec(memory_space=pltpu.VMEM)] * (len(args) - smem - hbm_in)
    return pl.pallas_call(
        kernel,
        out_shape=out,
        in_specs=specs,
        out_specs=jax.tree.map(lambda _: pl.BlockSpec(memory_space=pltpu.VMEM), out),
        scratch_shapes=list(scratch),
        compiler_params=pltpu.CompilerParams(vmem_limit_bytes=limit * 1024 * 1024),
        cost_estimate=pl.CostEstimate(flops=flops, bytes_accessed=2 * nbytes, transcendentals=0),
    )(*args)


def shape(dims, dtype=F32):
    return jax.ShapeDtypeStruct(dims, dtype)


def dot(a, b, ca, cb):
    return lax.dot_general(a, b, (((ca,), (cb,)), ((), ())), preferred_element_type=F32)


def relative_blocks(place_ref):
    x, zl, c = place_ref[0], place_ref[2], place_ref[4]
    spots = []
    for kc, kx, kz in itertools.product(range(NC), range(NX), range(NZL)):
        spot = (lax.bitwise_xor(c, kc) * NX + lax.bitwise_xor(x, kx)) * NZL + lax.bitwise_xor(zl, kz)
        spots.append(spot)
    return spots


def logits_kernel(place_ref, emb_ref, cent_ref, p_ref, stat_ref, cent_t_ref, old_ref, held_ref):
    rows, width = emb_ref.shape
    step = 256
    spots = relative_blocks(place_ref)
    size = cent_ref.shape[0] // len(spots)
    for i, spot in enumerate(spots):
        held_ref[i * size : (i + 1) * size, :] = cent_ref[pl.ds(pl.multiple_of(spot * size, 16), size), :]
    cent = held_ref[...]
    cent_t_ref[...] = cent.T
    old_ref[...] = cent[:size, :].astype(F32)
    cent_f = cent.astype(F32)
    half_sq = 0.5 * jnp.sum(cent_f * cent_f, axis=1, keepdims=True)
    tops, sums = [], []
    for start in range(0, rows, step):
        cross = dot(cent, emb_ref[start : start + step, :], 1, 1)
        logits = (cross - half_sq) * (3.0 / math.sqrt(width))
        top = jnp.max(logits, axis=0, keepdims=True)
        p = jnp.exp(logits - top)
        p_ref[:, start : start + step] = p
        tops.append(top)
        sums.append(jnp.sum(p, axis=0, keepdims=True))
    block = jnp.concatenate(
        [
            jnp.concatenate(tops, axis=1).reshape(rows // 128, 128),
            jnp.concatenate(sums, axis=1).reshape(rows // 128, 128),
        ],
        axis=0,
    )
    for i in range(stat_ref.shape[0]):
        stat_ref[i] = block


def weights_kernel(place_ref, p_ref, mine_ref, stat_ref, cent_t_ref, wb_ref, count_ref, *out_refs):
    y, zh = place_ref[1], place_ref[3]
    half = stat_ref.shape[1] // 2
    tops = stat_ref[:, :half, :]
    top = jnp.max(tops, axis=0)
    total = jnp.sum(stat_ref[:, half:, :] * jnp.exp(tops - top[None]), axis=0)
    scale = jnp.exp(mine_ref[0, :half, :] - top) / total
    scale = scale.reshape(1, p_ref.shape[1])
    w = p_ref[...] * scale
    count_ref[...] = jnp.broadcast_to(jnp.sum(w, axis=1, keepdims=True), count_ref.shape)
    wb_ref[...] = w.astype(BF16)
    share = out_refs[0].shape[0]
    for part in range(2):
        for k in range(NY):
            side = (1 - zh) if part == 0 else zh
            start = ((y + k) % NY) * (NZH * share) + side * share
            piece = cent_t_ref[pl.ds(pl.multiple_of(start, 16), share), :]
            out_refs[part * NY + k][...] = dot(piece, wb_ref[...], 1, 0)


def mass_kernel(wb_ref, count_ref, emb_ref, keep_ref, send_ref):
    half, width = keep_ref.shape[0], emb_ref.shape[1]
    for ref, start in ((send_ref, half), (keep_ref, 0)):
        ref[:, :width] = dot(wb_ref[start : start + half, :], emb_ref[...], 1, 0)
        ref[:, width:] = count_ref[start : start + half, :]


def turn_kernel(place_ref, after_ref, emb_ref, emb_t_ref, turned_ref):
    share = emb_t_ref.shape[0]
    turned_ref[...] = emb_ref[...].T
    first = (place_ref[1] * NZH + place_ref[3]) * share
    emb_t_ref[...] = turned_ref[pl.ds(pl.multiple_of(first, 16), share), :].astype(F32)


def halve_kernel(mine_ref, got_ref, keep_ref, send_ref):
    half = keep_ref.shape[0]
    keep_ref[...] = mine_ref[:half, :] + got_ref[:half, :]
    send_ref[...] = mine_ref[half:, :] + got_ref[half:, :]


def centroid_kernel(mine_ref, got_ref, old_ref, out_ref):
    rows, width = out_ref.shape
    total = mine_ref[...] + got_ref[...]
    out_ref[...] = (total[:, :width] + old_ref[...]) / (total[:, width : width + 1] + 1.0)


def after_kernel(after_ref, a_ref, out_ref):
    out_ref[...] = a_ref[...]


def add_kernel(a_ref, b_ref, c_ref, d_ref, out_ref):
    out_ref[...] = (a_ref[...] + b_ref[...]) + (c_ref[...] + d_ref[...])


def row_of_owner(owner):
    rest, zl = divmod(owner, NZL)
    x, core = divmod(rest, NC)
    return (x * NZL + zl) * NC + core


def pieces(v):
    hi = v.astype(BF16).astype(F32)
    rest = v - hi
    mid = rest.astype(BF16).astype(F32)
    return hi, mid, rest - mid


def codebook_kernel(
    place_ref, all_books_ref, emb_t_ref, a_ref, b_ref, c_ref, d_ref, e_ref, out_ref, books_ref, sem
):
    subspaces, depth, codes = books_ref.shape
    first = (place_ref[1] * NZH + place_ref[3]) * subspaces
    copy = pltpu.make_async_copy(all_books_ref.at[pl.ds(first, subspaces)], books_ref, sem)
    copy.start()
    copy.wait()
    rows = emb_t_ref.shape[1]
    ones = jnp.where(lax.broadcasted_iota(jnp.int32, (2 * depth, rows), 0) < 3, 1.0, 0.0)
    for m in range(subspaces):
        at = slice(m * depth, (m + 1) * depth)
        recon = a_ref[at, :] + b_ref[at, :] + c_ref[at, :] + d_ref[at, :] + e_ref[at, :]
        r = emb_t_ref[at, :] - recon
        r0, r1, r2 = pieces(r)
        book = books_ref[m]
        k0, k1, k2 = pieces(book)
        s0, s1, s2 = pieces(-0.5 * jnp.sum(book * book, axis=0, keepdims=True))
        zero = jnp.zeros((2 * depth - 3, codes), F32)
        left = jnp.concatenate([k0, k0, k1, k0, k2, k1, s0, s1, s2, zero], axis=0).astype(BF16)
        right = jnp.concatenate([r0, r1, r0, r2, r0, r1, ones], axis=0).astype(BF16)
        logits = dot(left, right, 0, 0)
        p = jnp.exp(logits - jnp.max(logits, axis=0, keepdims=True))
        inv = 1.0 / jnp.sum(p, axis=0, keepdims=True)
        q0, q1, q2 = pieces(r * inv)
        i0, i1, i2 = pieces(jnp.broadcast_to(inv, (depth, rows)))
        scaled = jnp.concatenate([q0, q1, q2, i0, i1, i2], axis=0).astype(BF16)
        p_hi = p.astype(BF16)
        high = dot(scaled, p_hi, 1, 1)
        mass = high[:depth] + (high[depth : 2 * depth] + high[2 * depth : 3 * depth])
        o = 3 * depth
        count = high[o : o + 1] + (high[o + depth : o + depth + 1] + high[o + 2 * depth : o + 2 * depth + 1])
        for d in range(depth):
            owner, slot = divmod(m * depth + d, 3)
            row = row_of_owner(owner)
            out_ref[row, slot : slot + 1, :] = mass[d : d + 1]
            out_ref[row, slot + 3 : slot + 4, :] = count


def update_kernel(place_ref, all_books_ref, parts_ref, out_ref, books_ref, sem):
    x, y, zl, zh, c = (place_ref[i] for i in range(5))
    share = books_ref.shape[0]
    first = pl.multiple_of((y * NZH + zh) * share, 8)
    copy = pltpu.make_async_copy(all_books_ref.at[pl.ds(first, share), :], books_ref, sem)
    copy.start()
    total = jnp.sum(parts_ref[...], axis=0)
    copy.wait()
    row = ((x * NC + c) * NZL + zl) * 3
    old = jnp.concatenate([books_ref[pl.ds(row + i, 1), :] for i in range(3)], axis=0)
    new = (total[:3] + old) / (total[3:6] + 1.0)
    tile = jnp.concatenate([new[:, :128], new[:, 128:], jnp.zeros((2, 128), F32)], axis=0)
    for i in range(out_ref.shape[0]):
        out_ref[i] = tile


def books_kernel(place_ref, mine_ref, theirs_ref, out_ref):
    core = place_ref[4]
    cents = NY * NZH
    size = NC * NZL * 3

    def place(refs):
        for kx, cent in itertools.product(range(NX), range(cents)):
            first = (kx * cents + cent) * NZL
            tiles = [ref[first + zl] for ref in refs for zl in range(NZL)]
            low = jnp.concatenate([tile[:3] for tile in tiles], axis=0)
            high = jnp.concatenate([tile[3:6] for tile in tiles], axis=0)
            row = (cent * NX + kx) * size
            out_ref[row : row + size, :128] = low
            out_ref[row : row + size, 128:] = high

    @pl.when(core == 0)
    def _():
        place((mine_ref, theirs_ref))

    @pl.when(core == 1)
    def _():
        place((theirs_ref, mine_ref))


def centroids_kernel(place_ref, mine_ref, theirs_ref, out_ref):
    spots = relative_blocks(place_ref)
    half = len(spots) // 2
    size = mine_ref.shape[0] // half
    for i, spot in enumerate(spots):
        ref = mine_ref if i < half else theirs_ref
        at = (i % half) * size
        out_ref[pl.ds(pl.multiple_of(spot * size, 8), size), :] = ref[at : at + size, :]


def body(embeddings, centroids, codebooks):
    rows_here, width = embeddings.shape
    held = centroids.shape[0]
    subspaces, depth, codes = codebooks.shape
    row_at = lax.axis_index("rows")
    cent_at = lax.axis_index("cent")
    x, zl, c = row_at // (NZL * NC), (row_at // NC) % NZL, row_at % NC
    y, zh = cent_at // NZH, cent_at % NZH
    place = jnp.stack([x, y, zl, zh, c]).astype(jnp.int32)
    cents = NY * NZH
    share = width // cents

    p, stat, cent_t, old = call(
        logits_kernel,
        (
            shape((held, rows_here)),
            shape((cents, 2 * rows_here // 128, 128)),
            shape((width, held), BF16),
            shape((held // (NC * NX * NZL), width)),
        ),
        (place, embeddings, centroids),
        smem=1,
        scratch=(pltpu.VMEM((held, width), BF16),),
        flops=2 * rows_here * held * width,
    )
    stats = lax.all_to_all(stat, "cent", 0, 0, tiled=True)
    outs = call(
        weights_kernel,
        (shape((held, rows_here), BF16), shape((held, 128))) + (shape((share, rows_here)),) * 8,
        (place, p, stat, stats, cent_t),
        smem=1,
        flops=2 * rows_here * held * width,
    )
    wb, counts, theirs, mine = outs[0], outs[1], outs[2:6], outs[6:10]
    steps = (1, -1, 2)
    got = [hop(theirs[k % NY], along_y(k)) for k in steps]
    got_mine = [hop(mine[k % NY], along_y(k)) for k in steps]
    total = call(add_kernel, shape((share, rows_here)), (theirs[0], *got))
    peer = hop(total, other_zh)
    emb_t = call(
        turn_kernel,
        shape((share, rows_here)),
        (place, total, embeddings),
        smem=1,
        hbm_in=1,
        scratch=(pltpu.VMEM((width, rows_here), BF16),),
    )

    keep, send = call(
        mass_kernel,
        (shape((held // 2, width + 128)),) * 2,
        (wb, counts, embeddings),
        flops=2 * rows_here * held * width,
    )
    for move in (other_core, along_x(2), along_x(1)):
        half = keep.shape[0] // 2
        got = hop(send, move)
        keep, send = call(halve_kernel, (shape((half, width + 128)),) * 2, (keep, got), limit=4)
    send, peer = lax.optimization_barrier((send, peer))
    got = hop(send, along_zl(2))
    peers = NX * NZL

    per = subspaces // cents
    sums = call(
        codebook_kernel,
        shape((NX * NZL * NC, 8, codes)),
        (place, codebooks, emb_t, mine[0], *got_mine, peer),
        smem=1,
        hbm_in=1,
        scratch=(pltpu.VMEM((per, depth, codes), F32), pltpu.SemaphoreType.DMA),
        flops=64 * rows_here * per * codes * 64,
    )
    sums, got = lax.optimization_barrier((sums, got))
    half = keep.shape[0] // 2
    keep, send = call(halve_kernel, (shape((half, width + 128)),) * 2, (keep, got), limit=4)
    new = call(
        centroid_kernel, shape((half, width)), (keep, hop(send, along_zl(1)), old), limit=4
    )
    new_z = jnp.concatenate([new] + [hop(new, along_zl(k)) for k in (1, 2, 3)], axis=0)
    all_parts = lax.all_to_all(sums, "rows", 0, 0, tiled=True)
    same_line = [
        [flat(xx, yy, zz, hh, cc) for yy in range(NY) for hh in range(NZH) for zz in range(NZL)]
        for xx in range(NX)
        for cc in range(NC)
    ]
    tile = call(
        update_kernel,
        shape((cents * NZL, 8, 128)),
        (place, codebooks.reshape(subspaces * depth, codes), all_parts),
        smem=1,
        hbm_in=1,
        scratch=(pltpu.VMEM((share, codes), F32), pltpu.SemaphoreType.DMA),
    )
    new_z = call(after_kernel, shape((4 * half, width)), (tile, new_z), hbm_in=1)
    new_x = jnp.concatenate([new_z] + [hop(new_z, along_x(k)) for k in (1, 2, 3)], axis=0)
    new_other = hop(new_x, other_core)
    new_centroids = call(
        centroids_kernel, shape((held, width)), (place, new_x, new_other), smem=1
    )
    line = lax.all_to_all(tile, BOTH, 0, 0, tiled=True, axis_index_groups=same_line)
    across = [
        [(xx * NZL + zz) * NC + cc for xx in range(NX)] for zz in range(NZL) for cc in range(NC)
    ]
    lines = jnp.broadcast_to(line[None], (NX,) + line.shape)
    tiles = lax.all_to_all(lines, "rows", 0, 0, tiled=True, axis_index_groups=across)
    tiles = tiles.reshape((NX * line.shape[0],) + line.shape[1:])
    tiles_other = hop(tiles, other_core)
    new_books = call(
        books_kernel, shape((subspaces * depth, codes)), (place, tiles, tiles_other), smem=1
    )
    return (new_centroids, new_books.reshape(codebooks.shape))


def solution(mesh):
    in_specs = (P("rows", None), P("cent", None), P())
    out_specs = (P("cent", None), P())
    return jax.shard_map(body, mesh=mesh, in_specs=in_specs, out_specs=out_specs, check_vma=False)
```

```python
import itertools
import math

import jax
import jax.numpy as jnp
from jax import lax
from jax.experimental import pallas as pl
from jax.experimental.pallas import tpu as pltpu
from jax.sharding import PartitionSpec as P

NX, NY, NZL, NZH, NC = 4, 4, 4, 2, 2
BOTH = ("rows", "cent")
F32, BF16 = jnp.float32, jnp.bfloat16


def flat(x, y, zl, zh, c):
    return ((x * NZL + zl) * NC + c) * (NY * NZH) + (y * NZH + zh)


def hop(value, move):
    pairs = []
    for place in itertools.product(range(NX), range(NY), range(NZL), range(NZH), range(NC)):
        pairs.append((flat(*place), flat(*move(*place))))
    return lax.ppermute(value, BOTH, pairs)


def along_x(k):
    return lambda x, y, zl, zh, c: (x ^ k, y, zl, zh, c)


def along_y(k):
    return lambda x, y, zl, zh, c: (x, (y + k) % NY, zl, zh, c)


def along_zl(k):
    return lambda x, y, zl, zh, c: (x, y, zl ^ k, zh, c)


def other_zh(x, y, zl, zh, c):
    return (x, y, zl, 1 - zh, c)


def other_core(x, y, zl, zh, c):
    return (x, y, zl, zh, 1 - c)


def call(kernel, out, args, smem=0, scratch=(), flops=0, limit=12, hbm_in=0):
    nbytes = sum(a.size * a.dtype.itemsize for a in args)
    specs = [pl.BlockSpec(memory_space=pltpu.SMEM)] * smem
    specs += [pl.BlockSpec(memory_space=pl.ANY)] * hbm_in
    specs += [pl.BlockSpec(memory_space=pltpu.VMEM)] * (len(args) - smem - hbm_in)
    return pl.pallas_call(
        kernel,
        out_shape=out,
        in_specs=specs,
        out_specs=jax.tree.map(lambda _: pl.BlockSpec(memory_space=pltpu.VMEM), out),
        scratch_shapes=list(scratch),
        compiler_params=pltpu.CompilerParams(vmem_limit_bytes=limit * 1024 * 1024),
        cost_estimate=pl.CostEstimate(flops=flops, bytes_accessed=2 * nbytes, transcendentals=0),
    )(*args)


def shape(dims, dtype=F32):
    return jax.ShapeDtypeStruct(dims, dtype)


def dot(a, b, ca, cb):
    return lax.dot_general(a, b, (((ca,), (cb,)), ((), ())), preferred_element_type=F32)


def relative_blocks(place_ref):
    x, zl, c = place_ref[0], place_ref[2], place_ref[4]
    spots = []
    for kc, kx, kz in itertools.product(range(NC), range(NX), range(NZL)):
        spot = (lax.bitwise_xor(c, kc) * NX + lax.bitwise_xor(x, kx)) * NZL + lax.bitwise_xor(zl, kz)
        spots.append(spot)
    return spots


def logits_kernel(place_ref, emb_ref, cent_ref, p_ref, stat_ref, cent_t_ref, old_ref, held_ref):
    rows, width = emb_ref.shape
    step = 256
    spots = relative_blocks(place_ref)
    size = cent_ref.shape[0] // len(spots)
    for i, spot in enumerate(spots):
        held_ref[i * size : (i + 1) * size, :] = cent_ref[pl.ds(pl.multiple_of(spot * size, 16), size), :]
    cent = held_ref[...]
    cent_t_ref[...] = cent.T
    old_ref[...] = cent[:size, :].astype(F32)
    cent_f = cent.astype(F32)
    half_sq = 0.5 * jnp.sum(cent_f * cent_f, axis=1, keepdims=True)
    tops, sums = [], []
    for start in range(0, rows, step):
        cross = dot(cent, emb_ref[start : start + step, :], 1, 1)
        logits = (cross - half_sq) * (3.0 / math.sqrt(width))
        top = jnp.max(logits, axis=0, keepdims=True)
        p = jnp.exp(logits - top)
        p_ref[:, start : start + step] = p
        tops.append(top)
        sums.append(jnp.sum(p, axis=0, keepdims=True))
    block = jnp.concatenate(
        [
            jnp.concatenate(tops, axis=1).reshape(rows // 128, 128),
            jnp.concatenate(sums, axis=1).reshape(rows // 128, 128),
        ],
        axis=0,
    )
    for i in range(stat_ref.shape[0]):
        stat_ref[i] = block


def weights_kernel(place_ref, p_ref, mine_ref, stat_ref, cent_t_ref, wb_ref, count_ref, *out_refs):
    y, zh = place_ref[1], place_ref[3]
    half = stat_ref.shape[1] // 2
    tops = stat_ref[:, :half, :]
    top = jnp.max(tops, axis=0)
    total = jnp.sum(stat_ref[:, half:, :] * jnp.exp(tops - top[None]), axis=0)
    scale = jnp.exp(mine_ref[0, :half, :] - top) / total
    scale = scale.reshape(1, p_ref.shape[1])
    w = p_ref[...] * scale
    count_ref[...] = jnp.broadcast_to(jnp.sum(w, axis=1, keepdims=True), count_ref.shape)
    wb_ref[...] = w.astype(BF16)
    share = out_refs[0].shape[0]
    for part in range(2):
        for k in range(NY):
            side = (1 - zh) if part == 0 else zh
            start = ((y + k) % NY) * (NZH * share) + side * share
            piece = cent_t_ref[pl.ds(pl.multiple_of(start, 16), share), :]
            out_refs[part * NY + k][...] = dot(piece, wb_ref[...], 1, 0)


def mass_kernel(wb_ref, count_ref, emb_ref, keep_ref, send_ref):
    half, width = keep_ref.shape[0], emb_ref.shape[1]
    for ref, start in ((send_ref, half), (keep_ref, 0)):
        ref[:, :width] = dot(wb_ref[start : start + half, :], emb_ref[...], 1, 0)
        ref[:, width:] = count_ref[start : start + half, :]


def turn_kernel(place_ref, after_ref, emb_ref, emb_t_ref, turned_ref):
    share = emb_t_ref.shape[0]
    turned_ref[...] = emb_ref[...].T
    first = (place_ref[1] * NZH + place_ref[3]) * share
    emb_t_ref[...] = turned_ref[pl.ds(pl.multiple_of(first, 16), share), :].astype(F32)


def halve_kernel(mine_ref, got_ref, keep_ref, send_ref):
    half = keep_ref.shape[0]
    keep_ref[...] = mine_ref[:half, :] + got_ref[:half, :]
    send_ref[...] = mine_ref[half:, :] + got_ref[half:, :]


def centroid_kernel(mine_ref, got_ref, old_ref, out_ref):
    rows, width = out_ref.shape
    total = mine_ref[...] + got_ref[...]
    out_ref[...] = (total[:, :width] + old_ref[...]) / (total[:, width : width + 1] + 1.0)


def after_kernel(after_ref, a_ref, out_ref):
    out_ref[...] = a_ref[...]


def add_kernel(a_ref, b_ref, c_ref, d_ref, out_ref):
    out_ref[...] = (a_ref[...] + b_ref[...]) + (c_ref[...] + d_ref[...])


def row_of_owner(owner):
    rest, zl = divmod(owner, NZL)
    x, core = divmod(rest, NC)
    return (x * NZL + zl) * NC + core


def pieces(v):
    hi = v.astype(BF16).astype(F32)
    rest = v - hi
    mid = rest.astype(BF16).astype(F32)
    return hi, mid, rest - mid


def codebook_kernel(
    place_ref, all_books_ref, emb_t_ref, a_ref, b_ref, c_ref, d_ref, e_ref, out_ref, books_ref, sem
):
    subspaces, depth, codes = books_ref.shape
    first = (place_ref[1] * NZH + place_ref[3]) * subspaces
    copy = pltpu.make_async_copy(all_books_ref.at[pl.ds(first, subspaces)], books_ref, sem)
    copy.start()
    copy.wait()
    rows = emb_t_ref.shape[1]
    ones = jnp.where(lax.broadcasted_iota(jnp.int32, (2 * depth, rows), 0) < 3, 1.0, 0.0)
    for m in range(subspaces):
        at = slice(m * depth, (m + 1) * depth)
        recon = a_ref[at, :] + b_ref[at, :] + c_ref[at, :] + d_ref[at, :] + e_ref[at, :]
        r = emb_t_ref[at, :] - recon
        r0, r1, r2 = pieces(r)
        book = books_ref[m]
        k0, k1, k2 = pieces(book)
        s0, s1, s2 = pieces(-0.5 * jnp.sum(book * book, axis=0, keepdims=True))
        zero = jnp.zeros((2 * depth - 3, codes), F32)
        left = jnp.concatenate([k0, k0, k1, k0, k2, k1, s0, s1, s2, zero], axis=0).astype(BF16)
        right = jnp.concatenate([r0, r1, r0, r2, r0, r1, ones], axis=0).astype(BF16)
        logits = dot(left, right, 0, 0)
        p = jnp.exp(logits - jnp.max(logits, axis=0, keepdims=True))
        inv = 1.0 / jnp.sum(p, axis=0, keepdims=True)
        q0, q1, q2 = pieces(r * inv)
        i0, i1, i2 = pieces(jnp.broadcast_to(inv, (depth, rows)))
        scaled = jnp.concatenate([q0, q1, q2, i0, i1, i2], axis=0).astype(BF16)
        p_hi = p.astype(BF16)
        high = dot(scaled, p_hi, 1, 1)
        mass = high[:depth] + (high[depth : 2 * depth] + high[2 * depth : 3 * depth])
        o = 3 * depth
        count = high[o : o + 1] + (high[o + depth : o + depth + 1] + high[o + 2 * depth : o + 2 * depth + 1])
        for d in range(depth):
            owner, slot = divmod(m * depth + d, 3)
            row = row_of_owner(owner)
            out_ref[row, slot : slot + 1, :] = mass[d : d + 1]
            out_ref[row, slot + 3 : slot + 4, :] = count


def update_kernel(place_ref, all_books_ref, parts_ref, out_ref, books_ref, sem):
    x, y, zl, zh, c = (place_ref[i] for i in range(5))
    share = books_ref.shape[0]
    first = pl.multiple_of((y * NZH + zh) * share, 8)
    copy = pltpu.make_async_copy(all_books_ref.at[pl.ds(first, share), :], books_ref, sem)
    copy.start()
    total = jnp.sum(parts_ref[...], axis=0)
    copy.wait()
    row = ((x * NC + c) * NZL + zl) * 3
    old = jnp.concatenate([books_ref[pl.ds(row + i, 1), :] for i in range(3)], axis=0)
    new = (total[:3] + old) / (total[3:6] + 1.0)
    tile = jnp.concatenate([new[:, :128], new[:, 128:], jnp.zeros((2, 128), F32)], axis=0)
    for i in range(out_ref.shape[0]):
        out_ref[i] = tile


def books_kernel(place_ref, mine_ref, theirs_ref, out_ref):
    core = place_ref[4]
    cents = NY * NZH
    size = NC * NZL * 3

    def place(refs):
        for kx, cent in itertools.product(range(NX), range(cents)):
            first = (kx * cents + cent) * NZL
            tiles = [ref[first + zl] for ref in refs for zl in range(NZL)]
            low = jnp.concatenate([tile[:3] for tile in tiles], axis=0)
            high = jnp.concatenate([tile[3:6] for tile in tiles], axis=0)
            row = (cent * NX + kx) * size
            out_ref[row : row + size, :128] = low
            out_ref[row : row + size, 128:] = high

    @pl.when(core == 0)
    def _():
        place((mine_ref, theirs_ref))

    @pl.when(core == 1)
    def _():
        place((theirs_ref, mine_ref))


def centroids_kernel(place_ref, mine_ref, theirs_ref, out_ref):
    spots = relative_blocks(place_ref)
    half = len(spots) // 2
    size = mine_ref.shape[0] // half
    for i, spot in enumerate(spots):
        ref = mine_ref if i < half else theirs_ref
        at = (i % half) * size
        out_ref[pl.ds(pl.multiple_of(spot * size, 8), size), :] = ref[at : at + size, :]


def body(embeddings, centroids, codebooks):
    rows_here, width = embeddings.shape
    held = centroids.shape[0]
    subspaces, depth, codes = codebooks.shape
    row_at = lax.axis_index("rows")
    cent_at = lax.axis_index("cent")
    x, zl, c = row_at // (NZL * NC), (row_at // NC) % NZL, row_at % NC
    y, zh = cent_at // NZH, cent_at % NZH
    place = jnp.stack([x, y, zl, zh, c]).astype(jnp.int32)
    cents = NY * NZH
    share = width // cents

    p, stat, cent_t, old = call(
        logits_kernel,
        (
            shape((held, rows_here)),
            shape((cents, 2 * rows_here // 128, 128)),
            shape((width, held), BF16),
            shape((held // (NC * NX * NZL), width)),
        ),
        (place, embeddings, centroids),
        smem=1,
        scratch=(pltpu.VMEM((held, width), BF16),),
        flops=2 * rows_here * held * width,
    )
    stats = lax.all_to_all(stat, "cent", 0, 0, tiled=True)
    outs = call(
        weights_kernel,
        (shape((held, rows_here), BF16), shape((held, 128))) + (shape((share, rows_here)),) * 8,
        (place, p, stat, stats, cent_t),
        smem=1,
        flops=2 * rows_here * held * width,
    )
    wb, counts, theirs, mine = outs[0], outs[1], outs[2:6], outs[6:10]
    steps = (2, 1, -1)
    got = [hop(theirs[k % NY], along_y(k)) for k in steps]
    got_mine = [hop(mine[k % NY], along_y(k)) for k in steps]
    total = call(add_kernel, shape((share, rows_here)), (theirs[0], *got))
    peer = hop(total, other_zh)
    emb_t = call(
        turn_kernel,
        shape((share, rows_here)),
        (place, total, embeddings),
        smem=1,
        hbm_in=1,
        scratch=(pltpu.VMEM((width, rows_here), BF16),),
    )

    keep, send = call(
        mass_kernel,
        (shape((held // 2, width + 128)),) * 2,
        (wb, counts, embeddings),
        flops=2 * rows_here * held * width,
    )
    for move in (other_core, along_x(2), along_x(1)):
        half = keep.shape[0] // 2
        got = hop(send, move)
        keep, send = call(halve_kernel, (shape((half, width + 128)),) * 2, (keep, got), limit=4)
    send, peer = lax.optimization_barrier((send, peer))
    got = hop(send, along_zl(2))
    peers = NX * NZL

    per = subspaces // cents
    sums = call(
        codebook_kernel,
        shape((NX * NZL * NC, 8, codes)),
        (place, codebooks, emb_t, mine[0], *got_mine, peer),
        smem=1,
        hbm_in=1,
        scratch=(pltpu.VMEM((per, depth, codes), F32), pltpu.SemaphoreType.DMA),
        flops=64 * rows_here * per * codes * 64,
    )
    sums, got = lax.optimization_barrier((sums, got))
    half = keep.shape[0] // 2
    keep, send = call(halve_kernel, (shape((half, width + 128)),) * 2, (keep, got), limit=4)
    new = call(
        centroid_kernel, shape((half, width)), (keep, hop(send, along_zl(1)), old), limit=4
    )
    new_z = jnp.concatenate([new] + [hop(new, along_zl(k)) for k in (1, 2, 3)], axis=0)
    all_parts = lax.all_to_all(sums, "rows", 0, 0, tiled=True)
    same_line = [
        [flat(xx, yy, zz, hh, cc) for yy in range(NY) for hh in range(NZH) for zz in range(NZL)]
        for xx in range(NX)
        for cc in range(NC)
    ]
    tile = call(
        update_kernel,
        shape((cents * NZL, 8, 128)),
        (place, codebooks.reshape(subspaces * depth, codes), all_parts),
        smem=1,
        hbm_in=1,
        scratch=(pltpu.VMEM((share, codes), F32), pltpu.SemaphoreType.DMA),
    )
    new_z = call(after_kernel, shape((4 * half, width)), (tile, new_z), hbm_in=1)
    new_x = jnp.concatenate([new_z] + [hop(new_z, along_x(k)) for k in (1, 2, 3)], axis=0)
    new_other = hop(new_x, other_core)
    new_centroids = call(
        centroids_kernel, shape((held, width)), (place, new_x, new_other), smem=1
    )
    line = lax.all_to_all(tile, BOTH, 0, 0, tiled=True, axis_index_groups=same_line)
    across = [
        [(xx * NZL + zz) * NC + cc for xx in range(NX)] for zz in range(NZL) for cc in range(NC)
    ]
    lines = jnp.broadcast_to(line[None], (NX,) + line.shape)
    tiles = lax.all_to_all(lines, "rows", 0, 0, tiled=True, axis_index_groups=across)
    tiles = tiles.reshape((NX * line.shape[0],) + line.shape[1:])
    tiles_other = hop(tiles, other_core)
    new_books = call(
        books_kernel, shape((subspaces * depth, codes)), (place, tiles, tiles_other), smem=1
    )
    return (new_centroids, new_books.reshape(codebooks.shape))


def solution(mesh):
    in_specs = (P("rows", None), P("cent", None), P())
    out_specs = (P("cent", None), P())
    return jax.shard_map(body, mesh=mesh, in_specs=in_specs, out_specs=out_specs, check_vma=False)
```
